256 devices in a mesh: rows: 64 (over z, x, core), cols: 4 (over y).
Axes of the slice: x: 4, y: 4, z: 8, core: 2. Of those that a mesh axis runs over, the one named last changes fastest.
Arguments:
- tiles: bfloat16 [64, 4, 32, 128, 128], P('rows', 'cols'), may hold values from -3 to 3
- tile_rows: int32 [64, 4, 32], P('rows', 'cols'), may hold values from 0 to 15
- tile_cols: int32 [64, 4, 32], P('rows', 'cols'), may hold values from 0 to 15
- tile_counts: int32 [64, 4], P('rows', 'cols'), may hold values from 16 to 32, as said below
- sketch: bfloat16 [4, 2048, 256], P('cols', 'rows'), may hold values from -6 to 6
Outputs:
- basis: float32 [131072, 256], P(('rows', 'cols'))
- factor: float32 [256, 256], replicated
The draws below stay inside these ranges and needn't reach their ends.
Inputs may be any that keep to these rules, and one draw needn't show every extreme that they name: The live slots of a slab and column group are its first tile_counts slots; some slab and group has all 32 slots live.
All inputs are finite; a program needn't handle non-finite values.
Results may differ from the reference program's by a relative error of at most 0.004.
Values may be sent and summed in bfloat16 or wider, within the bound.
A program may use at most 64 MiB of HBM per device.

```python
import jax
import jax.numpy as jnp
from jax import lax

TILE = 128
K = 256
ROUNDS = 2
TR = 16
CGT = 16
TILES = 32
GROUP = 2048
ROWS_TOTAL = 131072
COLS_TOTAL = 8192
N_ROWS = 64
N_COLS = 4


def draw_tiles(key, part):
    key = jax.random.fold_in(key, 11)
    shape = (N_ROWS, N_COLS, TILES, TILE, TILE)
    rise_rows = 3.0 ** (jnp.arange(N_ROWS, dtype=jnp.float32) / max(N_ROWS - 1, 1))
    rise_cols = 3.0 ** (jnp.arange(N_COLS, dtype=jnp.float32) / max(N_COLS - 1, 1))
    base = jnp.clip(jax.random.normal(key, shape, jnp.float32), -4.0, 4.0)
    rise = rise_rows[:, None] * rise_cols[None, :]
    values = base * rise[:, :, None, None, None] / 16.0
    return values.astype(jnp.bfloat16)


def draw_tile_counts(key, part):
    key = jax.random.fold_in(key, 7)
    counts = jax.random.randint(key, (N_ROWS * N_COLS,), TILES // 2, TILES + 1, dtype=jnp.int32)
    chosen = jax.random.randint(jax.random.fold_in(key, 1), (), 0, N_ROWS * N_COLS, dtype=jnp.int32)
    counts = counts.at[chosen].set(TILES)
    return counts.reshape(N_ROWS, N_COLS)


def plant(entries, key, least, high):
    shape = entries.shape
    spot = [jax.random.randint(jax.random.fold_in(key, axis), (), 0, shape[axis]) for axis in range(len(shape))]
    entries = entries.at[tuple(spot)].set(least)
    longest = shape.index(max(shape))
    spot[longest] = (spot[longest] + 1) % shape[longest]
    return entries.at[tuple(spot)].set(high)


def level_of(own_key, shape, cuts, smallest, top_value):
    def one(dim, blocks):
        draws = jax.random.uniform(jax.random.fold_in(jax.random.fold_in(own_key, 6), dim), (blocks,), jnp.float32, smallest / len(cuts), top_value / len(cuts))
        return jnp.repeat(jnp.exp(draws), shape[dim] // blocks).reshape((-1,) + (1,) * (len(shape) - dim - 1))

    level = one(*cuts[0])
    for cut in cuts[1:]:
        level = level * one(*cut)
    return level


def noise(own_key, shape, scale, limit, shards=(), kind=jnp.bfloat16):
    gain = level_of(own_key, shape, shards, -0.22, 0.18) if shards else 1.0
    values = jax.random.normal(own_key, shape, jnp.float32) * scale * gain
    return jnp.minimum(jnp.maximum(values, -limit), limit).astype(kind)


def setup_inputs(seed: int = 0) -> dict:
    key_list = jax.random.split(jax.random.key(seed), 6)
    tiles = draw_tiles(jax.random.fold_in(key_list[5], 71), 0)
    tile_rows = plant(jax.random.randint(key_list[1], (N_ROWS, N_COLS, TILES), 0, TR), jax.random.fold_in(key_list[1], 1), 0, TR - 1).astype(jnp.int32)
    tile_cols = plant(jax.random.randint(key_list[2], (N_ROWS, N_COLS, TILES), 0, CGT), jax.random.fold_in(key_list[2], 1), 0, CGT - 1).astype(jnp.int32)
    tile_counts = draw_tile_counts(jax.random.fold_in(key_list[5], 71), 0)
    sketch = noise(key_list[4], (N_COLS, GROUP, K), 1.0, 6.0, ((0, 4), (1, 64)))
    return {"tiles": tiles, "tile_rows": tile_rows, "tile_cols": tile_cols, "tile_counts": tile_counts, "sketch": sketch}


def local_plain(blocks, rows_idx, cols_idx, live, xgroup):
    width = blocks.shape[1]
    rank = xgroup.shape[-1]
    picked = xgroup.reshape(-1, width, rank)[cols_idx].astype(jnp.float32)
    prods = jnp.einsum('tij,tjk->tik', blocks.astype(jnp.float32), picked, precision=lax.Precision.HIGHEST)
    onehot = ((rows_idx[None, :] == jnp.arange(TR, dtype=jnp.int32)[:, None]) & live[None, :]).astype(jnp.float32)
    return jnp.einsum('rt,tik->rik', onehot, prods, precision=lax.Precision.HIGHEST).reshape(-1, rank)

def local_transposed(blocks, rows_idx, cols_idx, live, qslab):
    width = blocks.shape[1]
    rank = qslab.shape[-1]
    picked = qslab.reshape(-1, width, rank)[rows_idx].astype(jnp.float32)
    prods = jnp.einsum('tij,tik->tjk', blocks.astype(jnp.float32), picked, precision=lax.Precision.HIGHEST)
    onehot = ((cols_idx[None, :] == jnp.arange(CGT, dtype=jnp.int32)[:, None]) & live[None, :]).astype(jnp.float32)
    return jnp.einsum('ct,tjk->cjk', onehot, prods, precision=lax.Precision.HIGHEST).reshape(-1, rank)

def normalize(matrix, total):
    gram = jnp.dot(matrix.T, matrix, precision=lax.Precision.HIGHEST) / total
    lower = jnp.linalg.cholesky(gram)
    inverse = jax.scipy.linalg.solve_triangular(lower, jnp.eye(gram.shape[0], dtype=jnp.float32), lower=True)
    return (jnp.dot(matrix, inverse.T, precision=lax.Precision.HIGHEST), lower)

def reference(tiles, tile_rows, tile_cols, tile_counts, sketch):
    slots = tiles.shape[2]
    live = jnp.arange(slots, dtype=jnp.int32)[None, None, :] < tile_counts[:, :, None]
    rank = sketch.shape[-1]

    def plain(xgroups):

        def one_slab(items):
            blocks, rows_idx, cols_idx, alive = items
            parts = jax.vmap(local_plain)(blocks, rows_idx, cols_idx, alive, xgroups)
            return jnp.sum(parts, axis=0)
        return lax.map(one_slab, (tiles, tile_rows, tile_cols, live)).reshape(-1, rank)

    def transposed(qmatrix):
        qslabs = qmatrix.reshape(tiles.shape[0], -1, rank)

        def add_slab(total, items):
            blocks, rows_idx, cols_idx, alive, qslab = items
            parts = jax.vmap(local_transposed, in_axes=(0, 0, 0, 0, None))(blocks, rows_idx, cols_idx, alive, qslab)
            return (total + parts, None)
        start = jnp.zeros((tiles.shape[1], CGT * tiles.shape[3], rank), jnp.float32)
        total, unused = lax.scan(add_slab, start, (tiles, tile_rows, tile_cols, live, qslabs))
        return total.reshape(-1, rank)
    product = plain(sketch)
    result, lower = normalize(product, ROWS_TOTAL)
    for step in range(ROUNDS):
        image = transposed(result.astype(jnp.bfloat16))
        sketch_next, unused = normalize(image, COLS_TOTAL)
        product = plain(sketch_next.astype(jnp.bfloat16).reshape(tiles.shape[1], -1, rank))
        result, lower = normalize(product, ROWS_TOTAL)
    return (result, lower.T)
```

```python
import functools

import jax
import jax.numpy as jnp
from jax import lax
from jax.experimental import pallas as pl
from jax.experimental.pallas import tpu as pltpu
from jax.sharding import PartitionSpec as P

ROUNDS = 2
TR = 16
CGT = 16
TILE = 128
K = 256
SLOTS = 32
NZ = 8
NX = 4
NY = 4
PANEL = 64
COPIES = 80
F32 = jnp.float32
BF16 = jnp.bfloat16
HI = lax.Precision.HIGHEST
MESH = pl.DeviceIdType.MESH
VM = pltpu.VMEM
MIB = 1024 * 1024


def order_kernel(rows_ref, cols_ref, count_ref, byrow_ref, bycol_ref, cnt_ref):
    live = count_ref[0]

    def one(key_ref, other_ref, out_ref):
        for b in range(TR + 1):
            cnt_ref[b] = 0

        def count(t, carry):
            b = jnp.where(t < live, key_ref[t], TR)
            cnt_ref[b] = cnt_ref[b] + 1
            return carry

        lax.fori_loop(0, SLOTS, count, 0)
        at = jnp.int32(0)
        for b in range(TR + 1):
            n = cnt_ref[b]
            cnt_ref[b] = at
            if b < TR:
                out_ref[112 + b] = jnp.where(n > 0, 1, 0)
                out_ref[96 + b] = jnp.maximum(at + n - 1, 0)
            at = at + n

        def clear(t, carry):
            out_ref[64 + t] = 1
            return carry

        lax.fori_loop(0, SLOTS, clear, 0)
        for b in range(TR + 1):
            first = cnt_ref[b]

            @pl.when(first < SLOTS)
            def _():
                out_ref[64 + first] = 0

        def place(t, carry):
            b = jnp.where(t < live, key_ref[t], TR)
            k = cnt_ref[b]
            cnt_ref[b] = k + 1
            out_ref[k] = t
            out_ref[32 + k] = other_ref[t]
            return carry

        lax.fori_loop(0, SLOTS, place, 0)

    one(rows_ref, cols_ref, byrow_ref)
    one(cols_ref, rows_ref, bycol_ref)


def slot_orders(rows_idx, cols_idx, count):
    smem = pl.BlockSpec(memory_space=pltpu.SMEM)
    out = jax.ShapeDtypeStruct((128,), jnp.int32)
    return pl.pallas_call(
        order_kernel,
        name="orders",
        out_shape=(out, out),
        in_specs=[smem] * 3,
        out_specs=[smem] * 2,
        scratch_shapes=[pltpu.SMEM((TR + 1,), jnp.int32)],
    )(rows_idx, cols_idx, count)


def factor_kernel(scale, last, *refs):
    if last:
        g_ref, y_ref, q_ref, u_ref, x_ref, a_ref, e_ref = refs
    else:
        g_ref, x_ref, u_ref, a_ref, e_ref = refs
    n = K
    dn = (((0,), (0,)), ((), ()))
    a_ref[...] = g_ref[...] * scale
    row_i = lax.broadcasted_iota(jnp.int32, (n, n), 0)
    col_i = lax.broadcasted_iota(jnp.int32, (n, n), 1)
    e_ref[...] = jnp.where(row_i == col_i, 1.0, 0.0)
    sub = lax.broadcasted_iota(jnp.int32, (PANEL, 1), 0)
    for k in range(n // PANEL):
        lo = k * PANEL
        r = a_ref[lo : lo + PANEL, :]
        e = e_ref[lo : lo + PANEL, :]
        for j in range(PANEL):
            c = lo + j
            inv = lax.rsqrt(r[j : j + 1, c : c + 1])
            urow = r[j : j + 1, :] * inv
            xrow = e[j : j + 1, :] * inv
            f = jnp.where(sub > j, r[:, c : c + 1] * inv, 0.0)
            r = r - f * urow
            e = e - f * xrow
            u_ref[c : c + 1, :] = urow
            x_ref[c : c + 1, :] = xrow
        if lo + PANEL < n:
            u = u_ref[lo : lo + PANEL, :]
            x = x_ref[lo : lo + PANEL, :]
            a_ref[...] -= lax.dot_general(u, u, dn, precision=HI, preferred_element_type=F32)
            e_ref[...] -= lax.dot_general(u, x, dn, precision=HI, preferred_element_type=F32)
    if last:
        u_ref[...] = jnp.where(col_i >= row_i, u_ref[...], 0.0)
        q_ref[...] = apply_inverse(y_ref[...], x_ref[...])


def apply_inverse(share, inverse):
    return lax.dot_general(
        share, inverse, (((1,), (1,)), ((), ())), precision=HI, preferred_element_type=F32
    )


def factorize(gram, scale, share=None):
    vmem = pl.BlockSpec(memory_space=VM)
    square = jax.ShapeDtypeStruct((K, K), F32)
    buf = pltpu.VMEM((K, K), F32)
    params = pltpu.CompilerParams(vmem_limit_bytes=32 * MIB)
    if share is None:
        return pl.pallas_call(
            functools.partial(factor_kernel, scale, False),
            name="factor",
            out_shape=square,
            in_specs=[vmem],
            out_specs=vmem,
            scratch_shapes=[buf] * 3,
            compiler_params=params,
        )(gram)
    return pl.pallas_call(
        functools.partial(factor_kernel, scale, True),
        name="factor_apply",
        out_shape=(jax.ShapeDtypeStruct(share.shape, F32), square),
        in_specs=[vmem] * 2,
        out_specs=[vmem] * 2,
        scratch_shapes=[buf] * 3,
        compiler_params=params,
    )(gram, share)


class Net:
    def __init__(self, send, recv):
        self.send, self.recv, self.copies = send, recv, []

    def start(self, src, dst, device):
        k = len(self.copies)
        copy = pltpu.make_async_remote_copy(
            src_ref=src,
            dst_ref=dst,
            send_sem=self.send.at[k],
            recv_sem=self.recv.at[k],
            device_id=device,
            device_id_type=MESH,
        )
        copy.start()
        self.copies.append(copy)
        return copy

    def drain(self):
        for copy in self.copies:
            copy.wait_send()


def ring4(me):
    return lax.rem(me + 1, 4), lax.rem(me + 3, 4), lax.rem(me + 2, 4)


def gather4(net, loc, me, to, arrived=None):
    right, left, opp = ring4(me)
    r_a = net.start(loc(me, 0), loc(me, 0), to(right))
    l_b = net.start(loc(me, 1), loc(me, 1), to(left))
    r_b = net.start(loc(me, 1), loc(me, 1), to(right))
    l_a = net.start(loc(me, 0), loc(me, 0), to(left))
    if arrived is not None:
        arrived(me)
    r_a.wait_recv()
    f_a = net.start(loc(left, 0), loc(left, 0), to(right))
    l_b.wait_recv()
    f_b = net.start(loc(right, 1), loc(right, 1), to(left))
    r_b.wait_recv()
    if arrived is not None:
        arrived(left)
    l_a.wait_recv()
    if arrived is not None:
        arrived(right)
    f_a.wait_recv()
    f_b.wait_recv()
    if arrived is not None:
        arrived(opp)


def scatter4(net, src, me, to, buf, tmp, store, ready=None):
    right, left, opp = ring4(me)
    if ready is None:
        ready = lambda p: None
    ready(opp)
    a0 = net.start(src(opp, 0), buf.at[0], to(right))
    b0 = net.start(src(opp, 1), buf.at[1], to(left))
    ready(right)
    b1 = net.start(src(right, 1), buf.at[2], to(right))
    ready(left)
    a1 = net.start(src(left, 0), buf.at[3], to(left))
    a0.wait_recv()
    tmp[0] = src(right, 0)[...] + buf[0]
    a2 = net.start(tmp.at[0], buf.at[4], to(right))
    b0.wait_recv()
    tmp[1] = src(left, 1)[...] + buf[1]
    b2 = net.start(tmp.at[1], buf.at[5], to(left))
    ready(me)
    a1.wait_recv()
    b1.wait_recv()
    a2.wait_recv()
    store(0, src(me, 0)[...] + (buf[3] + buf[4]))
    b2.wait_recv()
    store(1, src(me, 1)[...] + (buf[2] + buf[5]))


def tile_products(tiles_ref, order_ref, load, prefix_ref, store, transposed):
    dn = (((0,), (0,)), ((), ())) if transposed else (((1,), (0,)), ((), ()))

    def step(k, acc):
        prod = lax.dot_general(
            tiles_ref[order_ref[k]], load(order_ref[32 + k]), dn, preferred_element_type=F32
        )
        acc = acc * order_ref[64 + k].astype(F32) + prod
        prefix_ref[k] = acc
        return acc

    lax.fori_loop(0, SLOTS, step, jnp.zeros((TILE, K), F32), unroll=4)
    for b in range(TR):
        store(b, prefix_ref[order_ref[96 + b]] * order_ref[112 + b].astype(F32))


def half_kernel(kind, *refs):
    if kind == "first":
        piece_ref, refs = refs[0], refs[1:]
    else:
        piece_ref, inverse_ref, refs = refs[0], refs[1], refs[2:]
    tiles_ref, order_ref, share_ref, gram_ref = refs[:4]
    x_ref, prefix_ref, part_ref = refs[4:7]
    g_ref, g1_ref, s1_ref, g2_ref, s2_ref, g3_ref, gf_ref = refs[7:14]
    send, recv = refs[14:16]
    buf_ref, tmp_ref = refs[16:18]
    transposed = kind == "columns"
    if transposed:
        r0_ref, c1_ref, c2_ref, rz_ref = refs[18:22]

    row, y = lax.axis_index("rows"), lax.axis_index("cols")
    core = lax.rem(row, 2)
    x = lax.rem(lax.div(row, 2), NX)
    z = lax.div(row, 2 * NX)
    q = lax.rem(row, 2 * NX)
    net = Net(send, recv)

    def at(z_, q_, y_):
        return (z_ * (2 * NX) + q_, y_)

    to_z = lambda p: at(p, q, y)
    to_q = lambda p: at(z, p, y)
    to_x = lambda p: at(z, p * 2 + core, y)
    to_y = lambda p: at(z, q, p)
    other_core = at(z, x * 2 + (1 - core), y)

    barrier = pltpu.get_barrier_semaphore()
    for d in range(1, NZ):
        pl.semaphore_signal(barrier, 1, device_id=to_z(lax.rem(z + d, NZ)), device_id_type=MESH)
    for d in range(1, 2 * NX):
        pl.semaphore_signal(barrier, 1, device_id=to_q(lax.rem(q + d, 2 * NX)), device_id_type=MESH)
    for d in range(1, NY):
        pl.semaphore_signal(barrier, 1, device_id=to_y(lax.rem(y + d, NY)), device_id_type=MESH)
    pl.semaphore_wait(barrier, NZ - 1 + 2 * NX - 1 + NY - 1)

    if transposed:
        mine = apply_inverse(piece_ref[...], inverse_ref[...]).astype(BF16)
        x_ref[y] = mine.reshape(2, 2, TILE, K)
        gather4(net, lambda p, h: x_ref.at[p, h], y, to_y)

        def load(b):
            return x_ref[b >> 2, (b >> 1) & 1, b & 1]

    else:
        xh, xl = lax.div(x, 2), lax.rem(x, 2)
        if kind == "first":
            x_ref[z, xh, xl, core] = piece_ref[...]
        else:
            x_ref[z, xh, xl, core] = apply_inverse(piece_ref[...], inverse_ref[...]).astype(BF16)
        spot = x_ref.at[z, xh, xl, core]
        copies = [net.start(spot, spot, to_z(lax.rem(z + d, NZ))) for d in range(1, NZ)]
        for copy in copies:
            copy.wait_recv()
        crossing = []

        def cross(p):
            spot = x_ref.at[:, lax.div(p, 2), lax.rem(p, 2), core]
            crossing.append(net.start(spot, spot, other_core))

        gather4(
            net,
            lambda p, h: x_ref.at[pl.ds(h * (NZ // 2), NZ // 2), lax.div(p, 2), lax.rem(p, 2), core],
            x,
            to_x,
            cross,
        )
        for copy in crossing:
            copy.wait_recv()

        def load(b):
            return x_ref[b >> 1, b & 1].reshape(TILE, K)

    if transposed:
        def keep(b, value):
            part_ref[b // 2, b % 2] = value.reshape(2, 2, 32, K)

        tile_products(tiles_ref, order_ref, load, prefix_ref, keep, True)
        right, left, opp = ring4(x)
        crossed = {}
        for name, p in (("opp", opp), ("right", right), ("left", left), ("me", x)):
            src = part_ref.at[:, lax.div(p, 2), lax.rem(p, 2), 1 - core]
            crossed[name] = net.start(src, r0_ref.at[p], other_core)
        names = iter(("opp", "right", "left", "me"))

        def ready(p):
            crossed[next(names)].wait_recv()
            c1_ref[p] = part_ref[:, lax.div(p, 2), lax.rem(p, 2), core] + r0_ref[p]

        def store(h, value):
            c2_ref[pl.ds(h * (NZ // 2), NZ // 2)] = value

        scatter4(
            net,
            lambda p, h: c1_ref.at[p, pl.ds(h * (NZ // 2), NZ // 2)],
            x,
            to_x,
            buf_ref,
            tmp_ref,
            store,
            ready,
        )
        copies = []
        for d in range(1, NZ):
            p = lax.rem(z + d, NZ)
            copies.append(net.start(c2_ref.at[p], rz_ref.at[d - 1], to_z(p)))
        total = c2_ref[z]
        for d, copy in enumerate(copies):
            copy.wait_recv()
            total = total + rz_ref[d]
        share = total
    else:
        def keep(b, value):
            part_ref[b // 4, (b // 2) % 2, b % 2] = value

        tile_products(tiles_ref, order_ref, load, prefix_ref, keep, False)

        def store(h, value):
            share_ref[h * 2 * TILE : (h + 1) * 2 * TILE, :] = value.reshape(2 * TILE, K)

        scatter4(
            net, lambda p, h: part_ref.at[p, h], y, to_y, buf_ref, tmp_ref, store
        )
        share = share_ref[...]
    if transposed:
        share_ref[...] = share

    gram = lax.dot_general(
        share, share, (((0,), (0,)), ((), ())), precision=HI, preferred_element_type=F32
    )
    g_ref[0] = gram[:, :128]
    g_ref[1] = gram[:, 128:]
    wide, thin = K // NX, K // NX // NZ
    copies = []
    for d in range(1, 2 * NX):
        p = lax.rem(q + d, 2 * NX)
        src = g_ref.at[lax.rem(p, 2), pl.ds(pl.multiple_of(lax.div(p, 2) * wide, wide), wide)]
        copies.append(net.start(src, g1_ref.at[d - 1], to_q(p)))
    total = g_ref[core, pl.ds(pl.multiple_of(x * wide, wide), wide)]
    for d, copy in enumerate(copies):
        copy.wait_recv()
        total = total + g1_ref[d]
    s1_ref[...] = total
    copies = []
    for d in range(1, NZ):
        p = lax.rem(z + d, NZ)
        src = s1_ref.at[pl.ds(pl.multiple_of(p * thin, thin), thin)]
        copies.append(net.start(src, g2_ref.at[d - 1], to_z(p)))
    total = s1_ref[pl.ds(pl.multiple_of(z * thin, thin), thin)]
    for d, copy in enumerate(copies):
        copy.wait_recv()
        total = total + g2_ref[d]
    g3_ref[y] = total
    copies = [
        net.start(g3_ref.at[y], g3_ref.at[y], to_y(lax.rem(y + d, NY))) for d in range(1, NY)
    ]
    for copy in copies:
        copy.wait_recv()
    total = (g3_ref[0] + g3_ref[1]) + (g3_ref[2] + g3_ref[3])
    at_thin = pl.ds(pl.multiple_of(x * wide + z * thin, thin), thin)
    gf_ref[core, at_thin] = total
    spot = gf_ref.at[core, at_thin]
    copies = [net.start(spot, spot, to_z(lax.rem(z + d, NZ))) for d in range(1, NZ)]
    for copy in copies:
        copy.wait_recv()
    spot = gf_ref.at[core, pl.ds(pl.multiple_of(x * wide, wide), wide)]
    copies = [net.start(spot, spot, to_q(lax.rem(q + d, 2 * NX))) for d in range(1, 2 * NX)]
    for copy in copies:
        copy.wait_recv()
    gram_ref[:, :128] = gf_ref[0]
    gram_ref[:, 128:] = gf_ref[1]
    net.drain()


COLLECTIVE = {"first": 1, "columns": 2, "rows": 3}


def half_round(kind, piece, inverse, tiles, order):
    transposed = kind == "columns"
    by_y = (NY, 2, 2, TILE, K)
    by_row = (NZ, 2, 2, 2, 32, K)
    share = (32, K) if transposed else (4 * TILE, K)
    half = (NZ // 2, 32, K) if transposed else (2, TILE, K)
    wide, thin = K // NX, K // NX // NZ
    scratch = [
        VM(by_y if transposed else by_row, BF16),
        VM((SLOTS, TILE, K), F32),
        VM(by_row if transposed else by_y, F32),
        VM((2, K, 128), F32),
        VM((2 * NX - 1, wide, 128), F32),
        VM((wide, 128), F32),
        VM((NZ - 1, thin, 128), F32),
        VM((thin, 128), F32),
        VM((NY, thin, 128), F32),
        VM((2, K, 128), F32),
        pltpu.SemaphoreType.DMA((COPIES,)),
        pltpu.SemaphoreType.DMA((COPIES,)),
        VM((6,) + half, F32),
        VM((2,) + half, F32),
    ]
    if transposed:
        scratch += [
            VM((NX, NZ, 32, K), F32),
            VM((NX, NZ, 32, K), F32),
            VM((NZ, 32, K), F32),
            VM((NZ - 1, 32, K), F32),
        ]
    operands = [piece] + ([] if inverse is None else [inverse]) + [tiles, order]
    vmem = pl.BlockSpec(memory_space=VM)
    return pl.pallas_call(
        functools.partial(half_kernel, kind),
        name="half_" + kind,
        out_shape=(jax.ShapeDtypeStruct(share, F32), jax.ShapeDtypeStruct((K, K), F32)),
        in_specs=[vmem] * (len(operands) - 1) + [pl.BlockSpec(memory_space=pltpu.SMEM)],
        out_specs=[vmem] * 2,
        scratch_shapes=scratch,
        compiler_params=pltpu.CompilerParams(
            collective_id=COLLECTIVE[kind], has_side_effects=True, vmem_limit_bytes=48 * MIB
        ),
    )(*operands)


def shards(tiles, tile_rows, tile_cols, tile_counts, sketch):
    blocks = tiles[0, 0]
    total_rows = TR * TILE * lax.axis_size("rows")
    total_cols = CGT * TILE * lax.axis_size("cols")
    by_row, by_col = slot_orders(tile_rows[0, 0], tile_cols[0, 0], tile_counts[0])
    share, gram = half_round("first", sketch[0], None, blocks, by_row)
    for step in range(ROUNDS):
        inverse = factorize(gram, 1.0 / total_rows)
        share, gram = half_round("columns", share, inverse, blocks, by_col)
        inverse = factorize(gram, 1.0 / total_cols)
        share, gram = half_round("rows", share, inverse, blocks, by_row)
    return factorize(gram, 1.0 / total_rows, share)


def solution(mesh):
    return jax.shard_map(
        shards,
        mesh=mesh,
        in_specs=(
            P("rows", "cols", None, None, None),
            P("rows", "cols", None),
            P("rows", "cols", None),
            P("rows", "cols"),
            P("cols", "rows", None),
        ),
        out_specs=(P(("rows", "cols"), None), P()),
        check_vma=False,
    )
```

```python
import functools

import jax
import jax.numpy as jnp
from jax import lax
from jax.experimental import pallas as pl
from jax.experimental.pallas import tpu as pltpu
from jax.sharding import PartitionSpec as P

ROUNDS = 2
TR = 16
CGT = 16
TILE = 128
K = 256
SLOTS = 32
NZ = 8
NX = 4
NY = 4
PANEL = 64
COPIES = 80
F32 = jnp.float32
BF16 = jnp.bfloat16
HI = lax.Precision.HIGHEST
MESH = pl.DeviceIdType.MESH
VM = pltpu.VMEM
MIB = 1024 * 1024


def order_kernel(rows_ref, cols_ref, count_ref, byrow_ref, bycol_ref, cnt_ref):
    live = count_ref[0]

    def one(key_ref, other_ref, out_ref):
        for b in range(TR + 1):
            cnt_ref[b] = 0

        def count(t, carry):
            b = jnp.where(t < live, key_ref[t], TR)
            cnt_ref[b] = cnt_ref[b] + 1
            return carry

        lax.fori_loop(0, SLOTS, count, 0)
        at = jnp.int32(0)
        for b in range(TR + 1):
            n = cnt_ref[b]
            cnt_ref[b] = at
            if b < TR:
                out_ref[112 + b] = jnp.where(n > 0, 1, 0)
                out_ref[96 + b] = jnp.maximum(at + n - 1, 0)
            at = at + n

        def clear(t, carry):
            out_ref[64 + t] = 1
            return carry

        lax.fori_loop(0, SLOTS, clear, 0)
        for b in range(TR + 1):
            first = cnt_ref[b]

            @pl.when(first < SLOTS)
            def _():
                out_ref[64 + first] = 0

        def place(t, carry):
            b = jnp.where(t < live, key_ref[t], TR)
            k = cnt_ref[b]
            cnt_ref[b] = k + 1
            out_ref[k] = t
            out_ref[32 + k] = other_ref[t]
            return carry

        lax.fori_loop(0, SLOTS, place, 0)

    one(rows_ref, cols_ref, byrow_ref)
    one(cols_ref, rows_ref, bycol_ref)


def slot_orders(rows_idx, cols_idx, count):
    smem = pl.BlockSpec(memory_space=pltpu.SMEM)
    out = jax.ShapeDtypeStruct((128,), jnp.int32)
    return pl.pallas_call(
        order_kernel,
        name="orders",
        out_shape=(out, out),
        in_specs=[smem] * 3,
        out_specs=[smem] * 2,
        scratch_shapes=[pltpu.SMEM((TR + 1,), jnp.int32)],
    )(rows_idx, cols_idx, count)


def spread(rows, q):
    return jnp.broadcast_to(rows[q : q + 1, :], (8, 128))


def factor_panel(lo, a_ref, e_ref, u_ref, x_ref):
    groups = PANEL // 8
    first = lo < 128
    a_half = (0, 1) if first else (1,)
    e_half = (0,) if first else (0, 1)
    n_a = len(a_half)
    sub = lax.broadcasted_iota(jnp.int32, (8, 128), 0)

    def rows_of(ref, g, halves):
        return [ref[lo + 8 * g : lo + 8 * g + 8, 128 * h : 128 * h + 128] for h in halves]

    rows = [rows_of(a_ref, g, a_half) + rows_of(e_ref, g, e_half) for g in range(groups)]
    for g in range(groups):
        c = (lo + 8 * g) % 128
        cols = [
            [jnp.broadcast_to(rows[i][0][:, c + q : c + q + 1], (8, 128)) for i in range(g, groups)]
            for q in range(8)
        ]
        done = []
        for q in range(8):
            inv = lax.rsqrt(spread(cols[q][0], q))
            cols[q] = [v * inv for v in cols[q]]
            for p in range(q + 1, 8):
                s = spread(cols[q][0], p)
                cols[p] = [v - w * s for v, w in zip(cols[p], cols[q])]
            row = [spread(v, q) for v in rows[g]]
            for w in range(q):
                s = spread(cols[w][0], q)
                row = [v - s * t for v, t in zip(row, done[w])]
            done.append([v * inv for v in row])
        out = done[0]
        for q in range(1, 8):
            out = [jnp.where(sub == q, v, o) for v, o in zip(done[q], out)]
        at = lo + 8 * g
        for h, v in zip(a_half, out[:n_a]):
            u_ref[at : at + 8, 128 * h : 128 * h + 128] = v
        for h, v in zip(e_half, out[n_a:]):
            x_ref[at : at + 8, 128 * h : 128 * h + 128] = v
        for i in range(g + 1, groups):
            for q in range(8):
                rows[i] = [v - cols[q][i - g] * t for v, t in zip(rows[i], done[q])]
    hi = lo + PANEL
    if hi < K:
        dn = (((0,), (0,)), ((), ()))
        a0 = 0 if hi < 128 else 128
        width = 128 if first else K
        u = u_ref[lo:hi, a0:]
        a_ref[a0:, a0:] -= lax.dot_general(u, u, dn, precision=HI, preferred_element_type=F32)
        e_ref[a0:, :width] -= lax.dot_general(
            u, x_ref[lo:hi, :width], dn, precision=HI, preferred_element_type=F32
        )


def factor_start(gram, a_ref, e_ref, u_ref, x_ref):
    a_ref[...] = gram
    row_i = lax.broadcasted_iota(jnp.int32, (K, K), 0)
    col_i = lax.broadcasted_iota(jnp.int32, (K, K), 1)
    e_ref[...] = jnp.where(row_i == col_i, 1.0, 0.0)
    x_ref[:128, 128:] = jnp.zeros((128, 128), F32)
    u_ref[128:, :128] = jnp.zeros((128, 128), F32)


def factor_kernel(scale, last, *refs):
    if last:
        g_ref, y_ref, q_ref, u_ref, x_ref, a_ref, e_ref = refs
    else:
        g_ref, x_ref, u_ref, a_ref, e_ref = refs
    factor_start(g_ref[...] * scale, a_ref, e_ref, u_ref, x_ref)
    for lo in range(0, K, PANEL):
        factor_panel(lo, a_ref, e_ref, u_ref, x_ref)
    if last:
        row_i = lax.broadcasted_iota(jnp.int32, (K, K), 0)
        col_i = lax.broadcasted_iota(jnp.int32, (K, K), 1)
        u_ref[...] = jnp.where(col_i >= row_i, u_ref[...], 0.0)
        q_ref[...] = apply_inverse(y_ref[...], x_ref[...])


def apply_inverse(share, inverse):
    return lax.dot_general(
        share, inverse, (((1,), (1,)), ((), ())), precision=HI, preferred_element_type=F32
    )


def factorize(gram, scale, share=None):
    vmem = pl.BlockSpec(memory_space=VM)
    square = jax.ShapeDtypeStruct((K, K), F32)
    buf = pltpu.VMEM((K, K), F32)
    params = pltpu.CompilerParams(vmem_limit_bytes=32 * MIB)
    if share is None:
        return pl.pallas_call(
            functools.partial(factor_kernel, scale, False),
            name="factor",
            out_shape=square,
            in_specs=[vmem],
            out_specs=vmem,
            scratch_shapes=[buf] * 3,
            compiler_params=params,
        )(gram)
    return pl.pallas_call(
        functools.partial(factor_kernel, scale, True),
        name="factor_apply",
        out_shape=(jax.ShapeDtypeStruct(share.shape, F32), square),
        in_specs=[vmem] * 2,
        out_specs=[vmem] * 2,
        scratch_shapes=[buf] * 3,
        compiler_params=params,
    )(gram, share)


class Net:
    def __init__(self, send, recv):
        self.send, self.recv, self.copies = send, recv, []

    def start(self, src, dst, device):
        k = len(self.copies)
        copy = pltpu.make_async_remote_copy(
            src_ref=src,
            dst_ref=dst,
            send_sem=self.send.at[k],
            recv_sem=self.recv.at[k],
            device_id=device,
            device_id_type=MESH,
        )
        copy.start()
        self.copies.append(copy)
        return copy

    def drain(self):
        for copy in self.copies:
            copy.wait_send()


def ring4(me):
    return lax.rem(me + 1, 4), lax.rem(me + 3, 4), lax.rem(me + 2, 4)


def gather4(net, loc, me, to, arrived=None):
    right, left, opp = ring4(me)
    r_a = net.start(loc(me, 0), loc(me, 0), to(right))
    l_b = net.start(loc(me, 1), loc(me, 1), to(left))
    r_b = net.start(loc(me, 1), loc(me, 1), to(right))
    l_a = net.start(loc(me, 0), loc(me, 0), to(left))
    if arrived is not None:
        arrived(me)
    r_a.wait_recv()
    f_a = net.start(loc(left, 0), loc(left, 0), to(right))
    l_b.wait_recv()
    f_b = net.start(loc(right, 1), loc(right, 1), to(left))
    r_b.wait_recv()
    if arrived is not None:
        arrived(left)
    l_a.wait_recv()
    if arrived is not None:
        arrived(right)
    f_a.wait_recv()
    f_b.wait_recv()
    if arrived is not None:
        arrived(opp)


def scatter4(net, src, me, to, buf, tmp, store, ready=None):
    right, left, opp = ring4(me)
    if ready is None:
        ready = lambda p: None
    ready(opp)
    a0 = net.start(src(opp, 0), buf.at[0], to(right))
    b0 = net.start(src(opp, 1), buf.at[1], to(left))
    ready(right)
    b1 = net.start(src(right, 1), buf.at[2], to(right))
    ready(left)
    a1 = net.start(src(left, 0), buf.at[3], to(left))
    a0.wait_recv()
    tmp[0] = src(right, 0)[...] + buf[0]
    a2 = net.start(tmp.at[0], buf.at[4], to(right))
    b0.wait_recv()
    tmp[1] = src(left, 1)[...] + buf[1]
    b2 = net.start(tmp.at[1], buf.at[5], to(left))
    ready(me)
    a1.wait_recv()
    b1.wait_recv()
    a2.wait_recv()
    store(0, src(me, 0)[...] + (buf[3] + buf[4]))
    b2.wait_recv()
    store(1, src(me, 1)[...] + (buf[2] + buf[5]))


def tile_products(tiles_ref, order_ref, load, prefix_ref, store, transposed):
    dn = (((0,), (0,)), ((), ())) if transposed else (((1,), (0,)), ((), ()))

    def step(k, acc):
        prod = lax.dot_general(
            tiles_ref[order_ref[k]], load(order_ref[32 + k]), dn, preferred_element_type=F32
        )
        acc = acc * order_ref[64 + k].astype(F32) + prod
        prefix_ref[k] = acc
        return acc

    lax.fori_loop(0, SLOTS, step, jnp.zeros((TILE, K), F32), unroll=4)
    for b in range(TR):
        store(b, prefix_ref[order_ref[96 + b]] * order_ref[112 + b].astype(F32))


def half_kernel(kind, *refs):
    if kind == "first":
        piece_ref, refs = refs[0], refs[1:]
    else:
        piece_ref, inverse_ref, refs = refs[0], refs[1], refs[2:]
    tiles_ref, order_ref, share_ref, gram_ref = refs[:4]
    x_ref, prefix_ref, part_ref = refs[4:7]
    g_ref, g1_ref, s1_ref, g2_ref, s2_ref, g3_ref, gf_ref = refs[7:14]
    send, recv = refs[14:16]
    buf_ref, tmp_ref = refs[16:18]
    transposed = kind == "columns"
    if transposed:
        r0_ref, c1_ref, c2_ref, rz_ref = refs[18:22]

    row, y = lax.axis_index("rows"), lax.axis_index("cols")
    core = lax.rem(row, 2)
    x = lax.rem(lax.div(row, 2), NX)
    z = lax.div(row, 2 * NX)
    q = lax.rem(row, 2 * NX)
    net = Net(send, recv)

    def at(z_, q_, y_):
        return (z_ * (2 * NX) + q_, y_)

    to_z = lambda p: at(p, q, y)
    to_q = lambda p: at(z, p, y)
    to_x = lambda p: at(z, p * 2 + core, y)
    to_y = lambda p: at(z, q, p)
    other_core = at(z, x * 2 + (1 - core), y)

    barrier = pltpu.get_barrier_semaphore()
    for d in range(1, NZ):
        pl.semaphore_signal(barrier, 1, device_id=to_z(lax.rem(z + d, NZ)), device_id_type=MESH)
    for d in range(1, 2 * NX):
        pl.semaphore_signal(barrier, 1, device_id=to_q(lax.rem(q + d, 2 * NX)), device_id_type=MESH)
    for d in range(1, NY):
        pl.semaphore_signal(barrier, 1, device_id=to_y(lax.rem(y + d, NY)), device_id_type=MESH)
    pl.semaphore_wait(barrier, NZ - 1 + 2 * NX - 1 + NY - 1)

    if transposed:
        mine = apply_inverse(piece_ref[...], inverse_ref[...]).astype(BF16)
        x_ref[y] = mine.reshape(2, 2, TILE, K)
        gather4(net, lambda p, h: x_ref.at[p, h], y, to_y)

        def load(b):
            return x_ref[b >> 2, (b >> 1) & 1, b & 1]

    else:
        xh, xl = lax.div(x, 2), lax.rem(x, 2)
        if kind == "first":
            x_ref[z, xh, xl, core] = piece_ref[...]
        else:
            x_ref[z, xh, xl, core] = apply_inverse(piece_ref[...], inverse_ref[...]).astype(BF16)
        spot = x_ref.at[z, xh, xl, core]
        copies = [net.start(spot, spot, to_z(lax.rem(z + d, NZ))) for d in range(1, NZ)]
        for copy in copies:
            copy.wait_recv()
        crossing = []

        def cross(p):
            spot = x_ref.at[:, lax.div(p, 2), lax.rem(p, 2), core]
            crossing.append(net.start(spot, spot, other_core))

        gather4(
            net,
            lambda p, h: x_ref.at[pl.ds(h * (NZ // 2), NZ // 2), lax.div(p, 2), lax.rem(p, 2), core],
            x,
            to_x,
            cross,
        )
        for copy in crossing:
            copy.wait_recv()

        def load(b):
            return x_ref[b >> 1, b & 1].reshape(TILE, K)

    if transposed:
        def keep(b, value):
            part_ref[b // 2, b % 2] = value.reshape(2, 2, 32, K)

        tile_products(tiles_ref, order_ref, load, prefix_ref, keep, True)
        right, left, opp = ring4(x)
        crossed = {}
        for name, p in (("opp", opp), ("right", right), ("left", left), ("me", x)):
            src = part_ref.at[:, lax.div(p, 2), lax.rem(p, 2), 1 - core]
            crossed[name] = net.start(src, r0_ref.at[p], other_core)
        names = iter(("opp", "right", "left", "me"))

        def ready(p):
            crossed[next(names)].wait_recv()
            c1_ref[p] = part_ref[:, lax.div(p, 2), lax.rem(p, 2), core] + r0_ref[p]

        def store(h, value):
            c2_ref[pl.ds(h * (NZ // 2), NZ // 2)] = value

        scatter4(
            net,
            lambda p, h: c1_ref.at[p, pl.ds(h * (NZ // 2), NZ // 2)],
            x,
            to_x,
            buf_ref,
            tmp_ref,
            store,
            ready,
        )
        copies = []
        for d in range(1, NZ):
            p = lax.rem(z + d, NZ)
            copies.append(net.start(c2_ref.at[p], rz_ref.at[d - 1], to_z(p)))
        total = c2_ref[z]
        for d, copy in enumerate(copies):
            copy.wait_recv()
            total = total + rz_ref[d]
        share = total
    else:
        def keep(b, value):
            part_ref[b // 4, (b // 2) % 2, b % 2] = value

        tile_products(tiles_ref, order_ref, load, prefix_ref, keep, False)

        def store(h, value):
            share_ref[h * 2 * TILE : (h + 1) * 2 * TILE, :] = value.reshape(2 * TILE, K)

        scatter4(
            net, lambda p, h: part_ref.at[p, h], y, to_y, buf_ref, tmp_ref, store
        )
        share = share_ref[...]
    if transposed:
        share_ref[...] = share

    gram = lax.dot_general(
        share, share, (((0,), (0,)), ((), ())), precision=HI, preferred_element_type=F32
    )
    g_ref[0] = gram[:, :128]
    g_ref[1] = gram[:, 128:]
    wide, thin = K // NX, K // NX // NZ
    copies = []
    for d in range(1, 2 * NX):
        p = lax.rem(q + d, 2 * NX)
        src = g_ref.at[lax.rem(p, 2), pl.ds(pl.multiple_of(lax.div(p, 2) * wide, wide), wide)]
        copies.append(net.start(src, g1_ref.at[d - 1], to_q(p)))
    total = g_ref[core, pl.ds(pl.multiple_of(x * wide, wide), wide)]
    for d, copy in enumerate(copies):
        copy.wait_recv()
        total = total + g1_ref[d]
    s1_ref[...] = total
    copies = []
    for d in range(1, NZ):
        p = lax.rem(z + d, NZ)
        src = s1_ref.at[pl.ds(pl.multiple_of(p * thin, thin), thin)]
        copies.append(net.start(src, g2_ref.at[d - 1], to_z(p)))
    total = s1_ref[pl.ds(pl.multiple_of(z * thin, thin), thin)]
    for d, copy in enumerate(copies):
        copy.wait_recv()
        total = total + g2_ref[d]
    g3_ref[y] = total
    copies = [
        net.start(g3_ref.at[y], g3_ref.at[y], to_y(lax.rem(y + d, NY))) for d in range(1, NY)
    ]
    for copy in copies:
        copy.wait_recv()
    total = (g3_ref[0] + g3_ref[1]) + (g3_ref[2] + g3_ref[3])
    at_thin = pl.ds(pl.multiple_of(x * wide + z * thin, thin), thin)
    gf_ref[core, at_thin] = total
    spot = gf_ref.at[core, at_thin]
    copies = [net.start(spot, spot, to_z(lax.rem(z + d, NZ))) for d in range(1, NZ)]
    for copy in copies:
        copy.wait_recv()
    spot = gf_ref.at[core, pl.ds(pl.multiple_of(x * wide, wide), wide)]
    copies = [net.start(spot, spot, to_q(lax.rem(q + d, 2 * NX))) for d in range(1, 2 * NX)]
    for copy in copies:
        copy.wait_recv()
    gram_ref[:, :128] = gf_ref[0]
    gram_ref[:, 128:] = gf_ref[1]
    net.drain()


COLLECTIVE = {"first": 1, "columns": 2, "rows": 3}


def half_round(kind, piece, inverse, tiles, order):
    transposed = kind == "columns"
    by_y = (NY, 2, 2, TILE, K)
    by_row = (NZ, 2, 2, 2, 32, K)
    share = (32, K) if transposed else (4 * TILE, K)
    half = (NZ // 2, 32, K) if transposed else (2, TILE, K)
    wide, thin = K // NX, K // NX // NZ
    scratch = [
        VM(by_y if transposed else by_row, BF16),
        VM((SLOTS, TILE, K), F32),
        VM(by_row if transposed else by_y, F32),
        VM((2, K, 128), F32),
        VM((2 * NX - 1, wide, 128), F32),
        VM((wide, 128), F32),
        VM((NZ - 1, thin, 128), F32),
        VM((thin, 128), F32),
        VM((NY, thin, 128), F32),
        VM((2, K, 128), F32),
        pltpu.SemaphoreType.DMA((COPIES,)),
        pltpu.SemaphoreType.DMA((COPIES,)),
        VM((6,) + half, F32),
        VM((2,) + half, F32),
    ]
    if transposed:
        scratch += [
            VM((NX, NZ, 32, K), F32),
            VM((NX, NZ, 32, K), F32),
            VM((NZ, 32, K), F32),
            VM((NZ - 1, 32, K), F32),
        ]
    operands = [piece] + ([] if inverse is None else [inverse]) + [tiles, order]
    vmem = pl.BlockSpec(memory_space=VM)
    return pl.pallas_call(
        functools.partial(half_kernel, kind),
        name="half_" + kind,
        out_shape=(jax.ShapeDtypeStruct(share, F32), jax.ShapeDtypeStruct((K, K), F32)),
        in_specs=[vmem] * (len(operands) - 1) + [pl.BlockSpec(memory_space=pltpu.SMEM)],
        out_specs=[vmem] * 2,
        scratch_shapes=scratch,
        compiler_params=pltpu.CompilerParams(
            collective_id=COLLECTIVE[kind], has_side_effects=True, vmem_limit_bytes=48 * MIB
        ),
    )(*operands)


def shards(tiles, tile_rows, tile_cols, tile_counts, sketch):
    blocks = tiles[0, 0]
    total_rows = TR * TILE * lax.axis_size("rows")
    total_cols = CGT * TILE * lax.axis_size("cols")
    by_row, by_col = slot_orders(tile_rows[0, 0], tile_cols[0, 0], tile_counts[0])
    share, gram = half_round("first", sketch[0], None, blocks, by_row)
    for step in range(ROUNDS):
        inverse = factorize(gram, 1.0 / total_rows)
        share, gram = half_round("columns", share, inverse, blocks, by_col)
        inverse = factorize(gram, 1.0 / total_cols)
        share, gram = half_round("rows", share, inverse, blocks, by_row)
    return factorize(gram, 1.0 / total_rows, share)


def solution(mesh):
    return jax.shard_map(
        shards,
        mesh=mesh,
        in_specs=(
            P("rows", "cols", None, None, None),
            P("rows", "cols", None),
            P("rows", "cols", None),
            P("rows", "cols"),
            P("cols", "rows", None),
        ),
        out_specs=(P(("rows", "cols"), None), P()),
        check_vma=False,
    )
```

```python
import functools

import jax
import jax.numpy as jnp
from jax import lax
from jax.experimental import pallas as pl
from jax.experimental.pallas import tpu as pltpu
from jax.sharding import PartitionSpec as P

ROUNDS = 2
TR = 16
CGT = 16
TILE = 128
K = 256
SLOTS = 32
NZ = 8
NX = 4
NY = 4
PANEL = 64
COPIES = 80
F32 = jnp.float32
BF16 = jnp.bfloat16
HI = lax.Precision.HIGHEST
MESH = pl.DeviceIdType.MESH
VM = pltpu.VMEM
MIB = 1024 * 1024


def order_kernel(rows_ref, cols_ref, count_ref, byrow_ref, bycol_ref, cnt_ref):
    live = count_ref[0]

    def one(key_ref, other_ref, out_ref):
        for b in range(TR + 1):
            cnt_ref[b] = 0

        def count(t, carry):
            b = jnp.where(t < live, key_ref[t], TR)
            cnt_ref[b] = cnt_ref[b] + 1
            return carry

        lax.fori_loop(0, SLOTS, count, 0)
        at = jnp.int32(0)
        for b in range(TR + 1):
            n = cnt_ref[b]
            cnt_ref[b] = at
            if b < TR:
                out_ref[112 + b] = jnp.where(n > 0, 1, 0)
                out_ref[96 + b] = jnp.maximum(at + n - 1, 0)
            at = at + n

        def clear(t, carry):
            out_ref[64 + t] = 1
            return carry

        lax.fori_loop(0, SLOTS, clear, 0)
        for b in range(TR + 1):
            first = cnt_ref[b]

            @pl.when(first < SLOTS)
            def _():
                out_ref[64 + first] = 0

        def place(t, carry):
            b = jnp.where(t < live, key_ref[t], TR)
            k = cnt_ref[b]
            cnt_ref[b] = k + 1
            out_ref[k] = t
            out_ref[32 + k] = other_ref[t]
            return carry

        lax.fori_loop(0, SLOTS, place, 0)

    one(rows_ref, cols_ref, byrow_ref)
    one(cols_ref, rows_ref, bycol_ref)


def slot_orders(rows_idx, cols_idx, count):
    smem = pl.BlockSpec(memory_space=pltpu.SMEM)
    out = jax.ShapeDtypeStruct((128,), jnp.int32)
    return pl.pallas_call(
        order_kernel,
        name="orders",
        out_shape=(out, out),
        in_specs=[smem] * 3,
        out_specs=[smem] * 2,
        scratch_shapes=[pltpu.SMEM((TR + 1,), jnp.int32)],
    )(rows_idx, cols_idx, count)


def spread(rows, q):
    return jnp.broadcast_to(rows[q : q + 1, :], (8, 128))


def factor_panel(lo, a_ref, e_ref, u_ref, x_ref):
    groups = PANEL // 8
    first = lo < 128
    a_half = (0, 1) if first else (1,)
    e_half = (0,) if first else (0, 1)
    n_a = len(a_half)
    sub = lax.broadcasted_iota(jnp.int32, (8, 128), 0)

    def rows_of(ref, g, halves):
        return [ref[lo + 8 * g : lo + 8 * g + 8, 128 * h : 128 * h + 128] for h in halves]

    rows = [rows_of(a_ref, g, a_half) + rows_of(e_ref, g, e_half) for g in range(groups)]
    for g in range(groups):
        c = (lo + 8 * g) % 128
        cols = [
            [jnp.broadcast_to(rows[i][0][:, c + q : c + q + 1], (8, 128)) for i in range(g, groups)]
            for q in range(8)
        ]
        done = []
        for q in range(8):
            inv = lax.rsqrt(spread(cols[q][0], q))
            cols[q] = [v * inv for v in cols[q]]
            for p in range(q + 1, 8):
                s = spread(cols[q][0], p)
                cols[p] = [v - w * s for v, w in zip(cols[p], cols[q])]
            row = [spread(v, q) for v in rows[g]]
            for w in range(q):
                s = spread(cols[w][0], q)
                row = [v - s * t for v, t in zip(row, done[w])]
            done.append([v * inv for v in row])
        out = done[0]
        for q in range(1, 8):
            out = [jnp.where(sub == q, v, o) for v, o in zip(done[q], out)]
        at = lo + 8 * g
        for h, v in zip(a_half, out[:n_a]):
            u_ref[at : at + 8, 128 * h : 128 * h + 128] = v
        for h, v in zip(e_half, out[n_a:]):
            x_ref[at : at + 8, 128 * h : 128 * h + 128] = v
        for i in range(g + 1, groups):
            for q in range(8):
                rows[i] = [v - cols[q][i - g] * t for v, t in zip(rows[i], done[q])]
    hi = lo + PANEL
    if hi < K:
        dn = (((0,), (0,)), ((), ()))
        a0 = 0 if hi < 128 else 128
        width = 128 if first else K
        u = u_ref[lo:hi, a0:]
        a_ref[a0:, a0:] -= lax.dot_general(u, u, dn, precision=HI, preferred_element_type=F32)
        e_ref[a0:, :width] -= lax.dot_general(
            u, x_ref[lo:hi, :width], dn, precision=HI, preferred_element_type=F32
        )


def factor_start(gram, a_ref, e_ref, u_ref, x_ref):
    a_ref[...] = gram
    row_i = lax.broadcasted_iota(jnp.int32, (K, K), 0)
    col_i = lax.broadcasted_iota(jnp.int32, (K, K), 1)
    e_ref[...] = jnp.where(row_i == col_i, 1.0, 0.0)
    x_ref[:128, 128:] = jnp.zeros((128, 128), F32)
    u_ref[128:, :128] = jnp.zeros((128, 128), F32)


def factor_kernel(scale, g_ref, y_ref, q_ref, u_ref, x_ref, a_ref, e_ref):
    factor_start(g_ref[...] * scale, a_ref, e_ref, u_ref, x_ref)
    for lo in range(0, K, PANEL):
        factor_panel(lo, a_ref, e_ref, u_ref, x_ref)
    row_i = lax.broadcasted_iota(jnp.int32, (K, K), 0)
    col_i = lax.broadcasted_iota(jnp.int32, (K, K), 1)
    u_ref[...] = jnp.where(col_i >= row_i, u_ref[...], 0.0)
    q_ref[...] = apply_inverse(y_ref[...], x_ref[...])


def apply_inverse(share, inverse):
    return lax.dot_general(
        share, inverse, (((1,), (1,)), ((), ())), precision=HI, preferred_element_type=F32
    )


def factorize(gram, scale, share):
    vmem = pl.BlockSpec(memory_space=VM)
    square = jax.ShapeDtypeStruct((K, K), F32)
    return pl.pallas_call(
        functools.partial(factor_kernel, scale),
        name="factor_apply",
        out_shape=(jax.ShapeDtypeStruct(share.shape, F32), square),
        in_specs=[vmem] * 2,
        out_specs=[vmem] * 2,
        scratch_shapes=[pltpu.VMEM((K, K), F32)] * 3,
        compiler_params=pltpu.CompilerParams(vmem_limit_bytes=32 * MIB),
    )(gram, share)


class Net:
    def __init__(self, send, recv):
        self.send, self.recv, self.copies = send, recv, []

    def start(self, src, dst, device):
        k = len(self.copies)
        copy = pltpu.make_async_remote_copy(
            src_ref=src,
            dst_ref=dst,
            send_sem=self.send.at[k],
            recv_sem=self.recv.at[k],
            device_id=device,
            device_id_type=MESH,
        )
        copy.start()
        self.copies.append(copy)
        return copy

    def drain(self):
        for copy in self.copies:
            copy.wait_send()


def ring4(me):
    return lax.rem(me + 1, 4), lax.rem(me + 3, 4), lax.rem(me + 2, 4)


def gather4(net, loc, me, to, arrived=None):
    arrived = arrived or (lambda p: None)
    right, left, opp = ring4(me)
    r_a = net.start(loc(me, 0), loc(me, 0), to(right))
    l_b = net.start(loc(me, 1), loc(me, 1), to(left))
    r_b = net.start(loc(me, 1), loc(me, 1), to(right))
    l_a = net.start(loc(me, 0), loc(me, 0), to(left))
    arrived(me)
    yield
    r_a.wait_recv()
    f_a = net.start(loc(left, 0), loc(left, 0), to(right))
    l_b.wait_recv()
    f_b = net.start(loc(right, 1), loc(right, 1), to(left))
    yield
    r_b.wait_recv()
    arrived(left)
    l_a.wait_recv()
    arrived(right)
    f_a.wait_recv()
    f_b.wait_recv()
    arrived(opp)


def gather_rows(net, x_ref, where, to_z, to_x, other_core):
    z, x, core = where
    spot = x_ref.at[z, lax.div(x, 2), lax.rem(x, 2), core]
    copies = [net.start(spot, spot, to_z(lax.rem(z + d, NZ))) for d in range(1, NZ)]
    yield
    for copy in copies:
        copy.wait_recv()
    crossing = []

    def cross(p):
        spot = x_ref.at[:, lax.div(p, 2), lax.rem(p, 2), core]
        crossing.append(net.start(spot, spot, other_core))

    def loc(p, h):
        return x_ref.at[pl.ds(h * (NZ // 2), NZ // 2), lax.div(p, 2), lax.rem(p, 2), core]

    yield from gather4(net, loc, x, to_x, cross)
    for copy in crossing:
        copy.wait_recv()


def scatter4(net, src, me, to, buf, tmp, store, ready=None):
    right, left, opp = ring4(me)
    ready = ready or (lambda p: None)
    ready(opp)
    a0 = net.start(src(opp, 0), buf.at[0], to(right))
    b0 = net.start(src(opp, 1), buf.at[1], to(left))
    ready(right)
    b1 = net.start(src(right, 1), buf.at[2], to(right))
    ready(left)
    a1 = net.start(src(left, 0), buf.at[3], to(left))
    yield
    a0.wait_recv()
    tmp[0] = src(right, 0)[...] + buf[0]
    a2 = net.start(tmp.at[0], buf.at[4], to(right))
    b0.wait_recv()
    tmp[1] = src(left, 1)[...] + buf[1]
    b2 = net.start(tmp.at[1], buf.at[5], to(left))
    ready(me)
    yield
    a1.wait_recv()
    b1.wait_recv()
    a2.wait_recv()
    store(0, src(me, 0)[...] + (buf[3] + buf[4]))
    b2.wait_recv()
    store(1, src(me, 1)[...] + (buf[2] + buf[5]))


def scatter_rows(net, part_ref, refs, where, to_z, to_x, other_core, out):
    z, x, core = where
    buf_ref, tmp_ref, r0_ref, c1_ref, c2_ref, rz_ref = refs
    right, left, opp = ring4(x)
    crossing = []
    for p in (opp, right, left, x):
        src = part_ref.at[:, lax.div(p, 2), lax.rem(p, 2), 1 - core]
        crossing.append(net.start(src, r0_ref.at[p], other_core))
    arriving = iter(crossing)
    yield

    def ready(p):
        next(arriving).wait_recv()
        c1_ref[p] = part_ref[:, lax.div(p, 2), lax.rem(p, 2), core] + r0_ref[p]

    def store(h, value):
        c2_ref[pl.ds(h * (NZ // 2), NZ // 2)] = value

    def src(p, h):
        return c1_ref.at[p, pl.ds(h * (NZ // 2), NZ // 2)]

    yield from scatter4(net, src, x, to_x, buf_ref, tmp_ref, store, ready)
    copies = []
    for d in range(1, NZ):
        p = lax.rem(z + d, NZ)
        copies.append(net.start(c2_ref.at[p], rz_ref.at[d - 1], to_z(p)))
    yield
    total = c2_ref[z]
    for d, copy in enumerate(copies):
        copy.wait_recv()
        total = total + rz_ref[d]
    out.append(total)


def gram_sum(net, share, refs, where, to_z, to_q, to_y):
    g_ref, g1_ref, s1_ref, g2_ref, s2_ref, g3_ref, gf_ref = refs
    z, x, core, q, y = where
    gram = lax.dot_general(
        share, share, (((0,), (0,)), ((), ())), precision=HI, preferred_element_type=F32
    )
    g_ref[0] = gram[:, :128]
    g_ref[1] = gram[:, 128:]
    wide, thin = K // NX, K // NX // NZ
    copies = []
    for d in range(1, 2 * NX):
        p = lax.rem(q + d, 2 * NX)
        src = g_ref.at[lax.rem(p, 2), pl.ds(pl.multiple_of(lax.div(p, 2) * wide, wide), wide)]
        copies.append(net.start(src, g1_ref.at[d - 1], to_q(p)))
    yield
    total = g_ref[core, pl.ds(pl.multiple_of(x * wide, wide), wide)]
    for d, copy in enumerate(copies):
        copy.wait_recv()
        total = total + g1_ref[d]
    s1_ref[...] = total
    copies = []
    for d in range(1, NZ):
        p = lax.rem(z + d, NZ)
        src = s1_ref.at[pl.ds(pl.multiple_of(p * thin, thin), thin)]
        copies.append(net.start(src, g2_ref.at[d - 1], to_z(p)))
    yield
    total = s1_ref[pl.ds(pl.multiple_of(z * thin, thin), thin)]
    for d, copy in enumerate(copies):
        copy.wait_recv()
        total = total + g2_ref[d]
    g3_ref[y] = total
    spot = g3_ref.at[y]
    copies = [net.start(spot, spot, to_y(lax.rem(y + d, NY))) for d in range(1, NY)]
    yield
    for copy in copies:
        copy.wait_recv()
    total = (g3_ref[0] + g3_ref[1]) + (g3_ref[2] + g3_ref[3])
    at_thin = pl.ds(pl.multiple_of(x * wide + z * thin, thin), thin)
    gf_ref[core, at_thin] = total
    spot = gf_ref.at[core, at_thin]
    copies = [net.start(spot, spot, to_z(lax.rem(z + d, NZ))) for d in range(1, NZ)]
    yield
    for copy in copies:
        copy.wait_recv()
    spot = gf_ref.at[core, pl.ds(pl.multiple_of(x * wide, wide), wide)]
    copies = [net.start(spot, spot, to_q(lax.rem(q + d, 2 * NX))) for d in range(1, 2 * NX)]
    yield
    for copy in copies:
        copy.wait_recv()


def tile_products(tiles_ref, order_ref, load, prefix_ref, store, transposed, twice):
    dn = (((0,), (0,)), ((), ())) if transposed else (((1,), (0,)), ((), ()))

    def step(k, acc):
        tile = tiles_ref[order_ref[k]]
        if twice:
            tile = jnp.concatenate([tile, tile], axis=0 if transposed else 1)
        prod = lax.dot_general(tile, load(order_ref[32 + k]), dn, preferred_element_type=F32)
        acc = acc * order_ref[64 + k].astype(F32) + prod
        prefix_ref[k] = acc
        return acc

    lax.fori_loop(0, SLOTS, step, jnp.zeros((TILE, K), F32), unroll=4)
    for b in range(TR):
        store(b, prefix_ref[order_ref[96 + b]] * order_ref[112 + b].astype(F32))


def two_parts(value):
    high = value.astype(BF16)
    return high, (value - high.astype(F32)).astype(BF16)


def step(*running):
    for stage in running:
        next(stage, None)


def half_kernel(kind, scale, *refs):
    refs = list(refs)

    def take(n):
        out, refs[:n] = refs[:n], []
        return out

    piece_ref, = take(1)
    if kind != "gram":
        tiles_ref, order_ref = take(2)
    out_ref, = take(1)
    send, recv = take(2)
    net = Net(send, recv)

    row, y = lax.axis_index("rows"), lax.axis_index("cols")
    core = lax.rem(row, 2)
    x = lax.rem(lax.div(row, 2), NX)
    z = lax.div(row, 2 * NX)
    q = lax.rem(row, 2 * NX)

    def at(z_, q_, y_):
        return (z_ * (2 * NX) + q_, y_)

    to_z = lambda p: at(p, q, y)
    to_q = lambda p: at(z, p, y)
    to_x = lambda p: at(z, p * 2 + core, y)
    to_y = lambda p: at(z, q, p)
    other_core = at(z, x * 2 + (1 - core), y)

    barrier = pltpu.get_barrier_semaphore()
    for d in range(1, NZ):
        pl.semaphore_signal(barrier, 1, device_id=to_z(lax.rem(z + d, NZ)), device_id_type=MESH)
    for d in range(1, 2 * NX):
        pl.semaphore_signal(barrier, 1, device_id=to_q(lax.rem(q + d, 2 * NX)), device_id_type=MESH)
    for d in range(1, NY):
        pl.semaphore_signal(barrier, 1, device_id=to_y(lax.rem(y + d, NY)), device_id_type=MESH)
    pl.semaphore_wait(barrier, NZ - 1 + 2 * NX - 1 + NY - 1)

    if kind != "first":
        gram_refs = take(7)
        gram = gram_sum(net, piece_ref[...], gram_refs, (z, x, core, q, y), to_z, to_q, to_y)
    if kind == "gram":
        for stage in gram:
            pass
        out_ref[:, :128] = gram_refs[-1][0]
        out_ref[:, 128:] = gram_refs[-1][1]
        net.drain()
        return

    x_ref, prefix_ref, part_ref, buf_ref, tmp_ref = take(5)
    out = []
    if kind == "columns":
        r0_ref, c1_ref, c2_ref, rz_ref = take(4)
        parts = [v.reshape(2, 2, TILE, K) for v in two_parts(piece_ref[...])]
        x_ref[y, :, :, 0] = parts[0]
        x_ref[y, :, :, 1] = parts[1]
        gather = gather4(net, lambda p, h: x_ref.at[p, h], y, to_y)
        scatter = scatter_rows(
            net,
            part_ref,
            (buf_ref, tmp_ref, r0_ref, c1_ref, c2_ref, rz_ref),
            (z, x, core),
            to_z,
            to_x,
            other_core,
            out,
        )

        def load(b):
            return x_ref[b >> 2, (b >> 1) & 1, b & 1].reshape(2 * TILE, K)

        def keep(b, value):
            part_ref[b // 2, b % 2] = value.reshape(2, 2, 32, K)

    else:
        xh, xl = lax.div(x, 2), lax.rem(x, 2)
        if kind == "first":
            x_ref[z, xh, xl, core, 0] = piece_ref[...]
        else:
            parts = two_parts(piece_ref[...])
            x_ref[z, xh, xl, core, 0] = parts[0]
            x_ref[z, xh, xl, core, 1] = parts[1]
        gather = gather_rows(net, x_ref, (z, x, core), to_z, to_x, other_core)

        def store(h, value):
            out.append(value.reshape(2 * TILE, K))

        scatter = scatter4(net, lambda p, h: part_ref.at[p, h], y, to_y, buf_ref, tmp_ref, store)

        def load(b):
            both = x_ref[b >> 1, b & 1]
            parts = [both[:, :, i].reshape(TILE, K) for i in range(both.shape[2])]
            return parts[0] if len(parts) == 1 else jnp.concatenate(parts, axis=0)

        def keep(b, value):
            part_ref[b // 4, (b // 2) % 2, b % 2] = value

    def products():
        tile_products(
            tiles_ref, order_ref, load, prefix_ref, keep, kind == "columns", kind != "first"
        )

    if kind == "first":
        for stage in gather:
            pass
        products()
        for stage in scatter:
            pass
        out_ref[: 2 * TILE, :] = out[0]
        out_ref[2 * TILE :, :] = out[1]
        net.drain()
        return

    a_ref, e_ref, u_ref, xi_ref = take(4)
    panels = [
        functools.partial(factor_panel, lo, a_ref, e_ref, u_ref, xi_ref)
        for lo in range(0, K, PANEL)
    ]
    if kind == "columns":
        step(gather, gram, gram, gather, gram)
        step(gather, gram)
        products()
        step(scatter, gram, scatter)
    else:
        step(gather, gram, gram, gather, gram, gather, gram, gather, gram)
        products()
        step(scatter)
    step(gram)
    full = jnp.concatenate([gram_refs[-1][0], gram_refs[-1][1]], axis=1)
    factor_start(full * scale, a_ref, e_ref, u_ref, xi_ref)
    for i, panel in enumerate(panels):
        panel()
        if i in ((0, 2) if kind == "columns" else (1,)):
            step(scatter)
    for stage in scatter:
        pass
    inverse = xi_ref[...]
    if kind == "columns":
        out_ref[...] = apply_inverse(out[0], inverse)
    else:
        out_ref[: 2 * TILE, :] = apply_inverse(out[0], inverse)
        out_ref[2 * TILE :, :] = apply_inverse(out[1], inverse)
    net.drain()


COLLECTIVE = {"first": 1, "columns": 2, "rows": 3, "gram": 4}


def half_round(kind, piece, scale=None, tiles=None, order=None):
    columns = kind == "columns"
    parts = 1 if kind == "first" else 2
    half = (NZ // 2, 32, K) if columns else (2, TILE, K)
    wide, thin = K // NX, K // NX // NZ
    scratch = [pltpu.SemaphoreType.DMA((COPIES,)), pltpu.SemaphoreType.DMA((COPIES,))]
    if kind != "first":
        scratch += [
            VM((2, K, 128), F32),
            VM((2 * NX - 1, wide, 128), F32),
            VM((wide, 128), F32),
            VM((NZ - 1, thin, 128), F32),
            VM((thin, 128), F32),
            VM((NY, thin, 128), F32),
            VM((2, K, 128), F32),
        ]
    if kind != "gram":
        if columns:
            scratch += [VM((NY, 2, 2, parts, TILE, K), BF16)]
        else:
            scratch += [VM((NZ, 2, 2, 2, parts, 32, K), BF16)]
        scratch += [
            VM((SLOTS, TILE, K), F32),
            VM((NZ, 2, 2, 2, 32, K) if columns else (NY, 2, 2, TILE, K), F32),
            VM((6,) + half, F32),
            VM((2,) + half, F32),
        ]
    if columns:
        scratch += [
            VM((NX, NZ, 32, K), F32),
            VM((NX, NZ, 32, K), F32),
            VM((NZ, 32, K), F32),
            VM((NZ - 1, 32, K), F32),
        ]
    if kind in ("columns", "rows"):
        scratch += [VM((K, K), F32)] * 4
    vmem = pl.BlockSpec(memory_space=VM)
    operands, specs = [piece], [vmem]
    if kind != "gram":
        operands += [tiles, order]
        specs += [vmem, pl.BlockSpec(memory_space=pltpu.SMEM)]
    rows = {"gram": K, "columns": 32}.get(kind, 4 * TILE)
    return pl.pallas_call(
        functools.partial(half_kernel, kind, scale),
        name="half_" + kind,
        out_shape=jax.ShapeDtypeStruct((rows, K), F32),
        in_specs=specs,
        out_specs=vmem,
        scratch_shapes=scratch,
        compiler_params=pltpu.CompilerParams(
            collective_id=COLLECTIVE[kind], has_side_effects=True, vmem_limit_bytes=48 * MIB
        ),
    )(*operands)


def shards(tiles, tile_rows, tile_cols, tile_counts, sketch):
    blocks = tiles[0, 0]
    total_rows = TR * TILE * lax.axis_size("rows")
    total_cols = CGT * TILE * lax.axis_size("cols")
    by_row, by_col = slot_orders(tile_rows[0, 0], tile_cols[0, 0], tile_counts[0])
    share = half_round("first", sketch[0], None, blocks, by_row)
    for step in range(ROUNDS):
        share = half_round("columns", share, 1.0 / total_rows, blocks, by_col)
        share = half_round("rows", share, 1.0 / total_cols, blocks, by_row)
    return factorize(half_round("gram", share), 1.0 / total_rows, share)


def solution(mesh):
    return jax.shard_map(
        shards,
        mesh=mesh,
        in_specs=(
            P("rows", "cols", None, None, None),
            P("rows", "cols", None),
            P("rows", "cols", None),
            P("rows", "cols"),
            P("cols", "rows", None),
        ),
        out_specs=(P(("rows", "cols"), None), P()),
        check_vma=False,
    )
```

```python
import functools

import jax
import jax.numpy as jnp
from jax import lax
from jax.experimental import pallas as pl
from jax.experimental.pallas import tpu as pltpu
from jax.sharding import PartitionSpec as P

ROUNDS = 2
TR = 16
CGT = 16
TILE = 128
K = 256
SLOTS = 32
NZ = 8
NX = 4
NY = 4
PANEL = 64
W = 128
F32 = jnp.float32
BF16 = jnp.bfloat16
HI = lax.Precision.HIGHEST
MESH = pl.DeviceIdType.MESH
VM = pltpu.VMEM
MIB = 1024 * 1024


def order_kernel(rows_ref, cols_ref, count_ref, byrow_ref, bycol_ref, cnt_ref):
    live = count_ref[0]

    def one(key_ref, other_ref, out_ref):
        for b in range(TR + 1):
            cnt_ref[b] = 0

        def count(t, carry):
            b = jnp.where(t < live, key_ref[t], TR)
            cnt_ref[b] = cnt_ref[b] + 1
            return carry

        lax.fori_loop(0, SLOTS, count, 0)
        at = jnp.int32(0)
        for b in range(TR + 1):
            n = cnt_ref[b]
            cnt_ref[b] = at
            if b < TR:
                out_ref[112 + b] = jnp.where(n > 0, 1, 0)
                out_ref[96 + b] = jnp.maximum(at + n - 1, 0)
            at = at + n

        def clear(t, carry):
            out_ref[64 + t] = 1
            return carry

        lax.fori_loop(0, SLOTS, clear, 0)
        for b in range(TR + 1):
            first = cnt_ref[b]

            @pl.when(first < SLOTS)
            def _():
                out_ref[64 + first] = 0

        def place(t, carry):
            b = jnp.where(t < live, key_ref[t], TR)
            k = cnt_ref[b]
            cnt_ref[b] = k + 1
            out_ref[k] = t
            out_ref[32 + k] = other_ref[t]
            return carry

        lax.fori_loop(0, SLOTS, place, 0)

    one(rows_ref, cols_ref, byrow_ref)
    one(cols_ref, rows_ref, bycol_ref)


def slot_orders(rows_idx, cols_idx, count):
    smem = pl.BlockSpec(memory_space=pltpu.SMEM)
    out = jax.ShapeDtypeStruct((128,), jnp.int32)
    return pl.pallas_call(
        order_kernel,
        name="orders",
        out_shape=(out, out),
        in_specs=[smem] * 3,
        out_specs=[smem] * 2,
        scratch_shapes=[pltpu.SMEM((TR + 1,), jnp.int32)],
    )(rows_idx, cols_idx, count)


def spread(rows, q):
    return jnp.broadcast_to(rows[q : q + 1, :], (8, 128))


def factor_panel(lo, a_ref, e_ref, u_ref, x_ref):
    groups = PANEL // 8
    first = lo < 128
    a_half = (0, 1) if first else (1,)
    e_half = (0,) if first else (0, 1)
    n_a = len(a_half)
    sub = lax.broadcasted_iota(jnp.int32, (8, 128), 0)

    def rows_of(ref, g, halves):
        return [ref[lo + 8 * g : lo + 8 * g + 8, 128 * h : 128 * h + 128] for h in halves]

    rows = [rows_of(a_ref, g, a_half) + rows_of(e_ref, g, e_half) for g in range(groups)]
    for g in range(groups):
        c = (lo + 8 * g) % 128
        cols = [
            [jnp.broadcast_to(rows[i][0][:, c + q : c + q + 1], (8, 128)) for i in range(g, groups)]
            for q in range(8)
        ]
        done = []
        for q in range(8):
            inv = lax.rsqrt(spread(cols[q][0], q))
            cols[q] = [v * inv for v in cols[q]]
            for p in range(q + 1, 8):
                s = spread(cols[q][0], p)
                cols[p] = [v - w * s for v, w in zip(cols[p], cols[q])]
            row = [spread(v, q) for v in rows[g]]
            for w in range(q):
                s = spread(cols[w][0], q)
                row = [v - s * t for v, t in zip(row, done[w])]
            done.append([v * inv for v in row])
        out = done[0]
        for q in range(1, 8):
            out = [jnp.where(sub == q, v, o) for v, o in zip(done[q], out)]
        at = lo + 8 * g
        for h, v in zip(a_half, out[:n_a]):
            u_ref[at : at + 8, 128 * h : 128 * h + 128] = v
        for h, v in zip(e_half, out[n_a:]):
            x_ref[at : at + 8, 128 * h : 128 * h + 128] = v
        for i in range(g + 1, groups):
            for q in range(8):
                rows[i] = [v - cols[q][i - g] * t for v, t in zip(rows[i], done[q])]
    hi = lo + PANEL
    if hi < K:
        dn = (((0,), (0,)), ((), ()))
        a0 = 0 if hi < 128 else 128
        width = 128 if first else K
        u = u_ref[lo:hi, a0:]
        a_ref[a0:, a0:] -= lax.dot_general(u, u, dn, precision=HI, preferred_element_type=F32)
        e_ref[a0:, :width] -= lax.dot_general(
            u, x_ref[lo:hi, :width], dn, precision=HI, preferred_element_type=F32
        )


def factor_start(gram, a_ref, e_ref, u_ref, x_ref):
    a_ref[...] = gram
    row_i = lax.broadcasted_iota(jnp.int32, (K, K), 0)
    col_i = lax.broadcasted_iota(jnp.int32, (K, K), 1)
    e_ref[...] = jnp.where(row_i == col_i, 1.0, 0.0)
    x_ref[:128, 128:] = jnp.zeros((128, 128), F32)
    u_ref[128:, :128] = jnp.zeros((128, 128), F32)


def factor_kernel(scale, g_ref, y_ref, q_ref, u_ref, x_ref, a_ref, e_ref):
    factor_start(g_ref[...] * scale, a_ref, e_ref, u_ref, x_ref)
    for lo in range(0, K, PANEL):
        factor_panel(lo, a_ref, e_ref, u_ref, x_ref)
    row_i = lax.broadcasted_iota(jnp.int32, (K, K), 0)
    col_i = lax.broadcasted_iota(jnp.int32, (K, K), 1)
    u_ref[...] = jnp.where(col_i >= row_i, u_ref[...], 0.0)
    q_ref[...] = apply_inverse(y_ref[...], x_ref[...])


def apply_inverse(share, inverse):
    return lax.dot_general(
        share, inverse, (((1,), (1,)), ((), ())), precision=HI, preferred_element_type=F32
    )


def factorize(gram, scale, share):
    vmem = pl.BlockSpec(memory_space=VM)
    square = jax.ShapeDtypeStruct((K, K), F32)
    return pl.pallas_call(
        functools.partial(factor_kernel, scale),
        name="factor_apply",
        out_shape=(jax.ShapeDtypeStruct(share.shape, F32), square),
        in_specs=[vmem] * 2,
        out_specs=[vmem] * 2,
        scratch_shapes=[pltpu.VMEM((K, K), F32)] * 3,
        compiler_params=pltpu.CompilerParams(vmem_limit_bytes=32 * MIB),
    )(gram, share)


class Net:
    def __init__(self, send, recv, base):
        self.send, self.recv, self.base, self.copies = send, recv, base, []

    def start(self, src, dst, device):
        k = self.base + len(self.copies)
        copy = pltpu.make_async_remote_copy(
            src_ref=src,
            dst_ref=dst,
            send_sem=self.send.at[k],
            recv_sem=self.recv.at[k],
            device_id=device,
            device_id_type=MESH,
        )
        copy.start()
        self.copies.append(copy)
        return copy

    def drain(self):
        for copy in self.copies:
            copy.wait_send()


def ring4(me):
    return lax.rem(me + 1, 4), lax.rem(me + 3, 4), lax.rem(me + 2, 4)


def gather4(net, loc, me, to, arrived=None):
    arrived = arrived or (lambda p: None)
    right, left, opp = ring4(me)
    r_a = net.start(loc(me, 0), loc(me, 0), to(right))
    l_b = net.start(loc(me, 1), loc(me, 1), to(left))
    r_b = net.start(loc(me, 1), loc(me, 1), to(right))
    l_a = net.start(loc(me, 0), loc(me, 0), to(left))
    arrived(me)
    yield
    r_a.wait_recv()
    f_a = net.start(loc(left, 0), loc(left, 0), to(right))
    l_b.wait_recv()
    f_b = net.start(loc(right, 1), loc(right, 1), to(left))
    yield
    r_b.wait_recv()
    arrived(left)
    l_a.wait_recv()
    arrived(right)
    f_a.wait_recv()
    f_b.wait_recv()
    arrived(opp)


def gather_rows(net, x_ref, where, to_z, to_x, other_core):
    z, x, core = where
    spot = x_ref.at[z, lax.div(x, 2), lax.rem(x, 2), core]
    copies = [net.start(spot, spot, to_z(lax.rem(z + d, NZ))) for d in range(1, NZ)]
    yield
    for copy in copies:
        copy.wait_recv()
    crossing = []

    def cross(p):
        spot = x_ref.at[:, lax.div(p, 2), lax.rem(p, 2), core]
        crossing.append(net.start(spot, spot, other_core))

    def loc(p, h):
        return x_ref.at[pl.ds(h * (NZ // 2), NZ // 2), lax.div(p, 2), lax.rem(p, 2), core]

    yield from gather4(net, loc, x, to_x, cross)
    for copy in crossing:
        copy.wait_recv()


def scatter4(net, src, me, to, buf, tmp, store, ready=None):
    right, left, opp = ring4(me)
    ready = ready or (lambda p: None)
    ready(opp)
    a0 = net.start(src(opp, 0), buf.at[0], to(right))
    b0 = net.start(src(opp, 1), buf.at[1], to(left))
    ready(right)
    b1 = net.start(src(right, 1), buf.at[2], to(right))
    ready(left)
    a1 = net.start(src(left, 0), buf.at[3], to(left))
    yield
    a0.wait_recv()
    tmp[0] = src(right, 0)[...] + buf[0]
    a2 = net.start(tmp.at[0], buf.at[4], to(right))
    b0.wait_recv()
    tmp[1] = src(left, 1)[...] + buf[1]
    b2 = net.start(tmp.at[1], buf.at[5], to(left))
    ready(me)
    yield
    a1.wait_recv()
    b1.wait_recv()
    a2.wait_recv()
    store(0, src(me, 0)[...] + (buf[3] + buf[4]))
    b2.wait_recv()
    store(1, src(me, 1)[...] + (buf[2] + buf[5]))


def scatter_rows(net, part_ref, refs, where, to_z, to_x, other_core, out):
    z, x, core = where
    buf_ref, tmp_ref, r0_ref, c1_ref, c2_ref, rz_ref = refs
    right, left, opp = ring4(x)
    crossing = []
    for p in (opp, right, left, x):
        src = part_ref.at[:, lax.div(p, 2), lax.rem(p, 2), 1 - core]
        crossing.append(net.start(src, r0_ref.at[p], other_core))
    arriving = iter(crossing)
    yield

    def ready(p):
        next(arriving).wait_recv()
        c1_ref[p] = part_ref[:, lax.div(p, 2), lax.rem(p, 2), core] + r0_ref[p]

    def store(h, value):
        c2_ref[pl.ds(h * (NZ // 2), NZ // 2)] = value

    def src(p, h):
        return c1_ref.at[p, pl.ds(h * (NZ // 2), NZ // 2)]

    yield from scatter4(net, src, x, to_x, buf_ref, tmp_ref, store, ready)
    copies = []
    for d in range(1, NZ):
        p = lax.rem(z + d, NZ)
        copies.append(net.start(c2_ref.at[p], rz_ref.at[d - 1], to_z(p)))
    yield
    total = c2_ref[z]
    for d, copy in enumerate(copies):
        copy.wait_recv()
        total = total + rz_ref[d]
    out.append(total)


def gram_sum(net, share, refs, where, to_z, to_q, to_y):
    g_ref, g1_ref, s1_ref, g2_ref, s2_ref, g3_ref, gf_ref = refs
    z, x, core, q, y = where
    gram = lax.dot_general(
        share, share, (((0,), (0,)), ((), ())), precision=HI, preferred_element_type=F32
    )
    g_ref[0] = gram[:, :128]
    g_ref[1] = gram[:, 128:]
    wide, thin = K // NX, K // NX // NZ
    copies = []
    for d in range(1, 2 * NX):
        p = lax.rem(q + d, 2 * NX)
        src = g_ref.at[lax.rem(p, 2), pl.ds(pl.multiple_of(lax.div(p, 2) * wide, wide), wide)]
        copies.append(net.start(src, g1_ref.at[d - 1], to_q(p)))
    yield
    total = g_ref[core, pl.ds(pl.multiple_of(x * wide, wide), wide)]
    for d, copy in enumerate(copies):
        copy.wait_recv()
        total = total + g1_ref[d]
    s1_ref[...] = total
    copies = []
    for d in range(1, NZ):
        p = lax.rem(z + d, NZ)
        src = s1_ref.at[pl.ds(pl.multiple_of(p * thin, thin), thin)]
        copies.append(net.start(src, g2_ref.at[d - 1], to_z(p)))
    yield
    total = s1_ref[pl.ds(pl.multiple_of(z * thin, thin), thin)]
    for d, copy in enumerate(copies):
        copy.wait_recv()
        total = total + g2_ref[d]
    g3_ref[y] = total
    spot = g3_ref.at[y]
    copies = [net.start(spot, spot, to_y(lax.rem(y + d, NY))) for d in range(1, NY)]
    yield
    for copy in copies:
        copy.wait_recv()
    total = (g3_ref[0] + g3_ref[1]) + (g3_ref[2] + g3_ref[3])
    at_thin = pl.ds(pl.multiple_of(x * wide + z * thin, thin), thin)
    gf_ref[core, at_thin] = total
    spot = gf_ref.at[core, at_thin]
    copies = [net.start(spot, spot, to_z(lax.rem(z + d, NZ))) for d in range(1, NZ)]
    yield
    for copy in copies:
        copy.wait_recv()
    spot = gf_ref.at[core, pl.ds(pl.multiple_of(x * wide, wide), wide)]
    copies = [net.start(spot, spot, to_q(lax.rem(q + d, 2 * NX))) for d in range(1, 2 * NX)]
    yield
    for copy in copies:
        copy.wait_recv()


def tile_products(tiles_ref, order_ref, load, prefix_ref, store, transposed, twice):
    dn = (((0,), (0,)), ((), ())) if transposed else (((1,), (0,)), ((), ()))

    def step(k, acc):
        tile = tiles_ref[order_ref[k]]
        if twice:
            tile = jnp.concatenate([tile, tile], axis=0 if transposed else 1)
        prod = lax.dot_general(tile, load(order_ref[32 + k]), dn, preferred_element_type=F32)
        acc = acc * order_ref[64 + k].astype(F32) + prod
        prefix_ref[k] = acc
        return acc

    lax.fori_loop(0, SLOTS, step, jnp.zeros((TILE, W), F32), unroll=8)
    for b in range(TR):
        store(b, prefix_ref[order_ref[96 + b]] * order_ref[112 + b].astype(F32))


def two_parts(value):
    high = value.astype(BF16)
    return high, (value - high.astype(F32)).astype(BF16)


def step(*running):
    for stage in running:
        next(stage, None)


def scratch_shapes():
    wide, thin = K // NX, K // NX // NZ
    shapes = {
        "x_first0": ((NZ, 2, 2, 2, 1, 32, W), BF16),
        "x_first1": ((NZ, 2, 2, 2, 1, 32, W), BF16),
        "x_rows0": ((NZ, 2, 2, 2, 2, 32, W), BF16),
        "x_rows1": ((NZ, 2, 2, 2, 2, 32, W), BF16),
        "x_columns0": ((NY, 2, 2, 2, TILE, W), BF16),
        "x_columns1": ((NY, 2, 2, 2, TILE, W), BF16),
        "prefix": ((SLOTS, TILE, W), F32),
        "part_rows": ((2, NY, 2, 2, TILE, W), F32),
        "part_columns": ((2, NZ, 2, 2, 2, 32, W), F32),
        "buf_rows": ((2, 6, 2, TILE, W), F32),
        "tmp_rows": ((2, 2, 2, TILE, W), F32),
        "buf_columns": ((2, 6, NZ // 2, 32, W), F32),
        "tmp_columns": ((2, 2, NZ // 2, 32, W), F32),
        "r0": ((2, NX, NZ, 32, W), F32),
        "c1": ((2, NX, NZ, 32, W), F32),
        "c2": ((2, NZ, 32, W), F32),
        "rz": ((2, NZ - 1, 32, W), F32),
        "g": ((2, 2, K, 128), F32),
        "g1": ((2, 2 * NX - 1, wide, 128), F32),
        "s1": ((2, wide, 128), F32),
        "g2": ((2, NZ - 1, thin, 128), F32),
        "s2": ((2, thin, 128), F32),
        "g3": ((2, NY, thin, 128), F32),
        "gf": ((2, 2, K, 128), F32),
        "a": ((K, K), F32),
        "e": ((K, K), F32),
        "u": ((K, K), F32),
        "inverse": ((K, K), F32),
        "y_share": ((4 * TILE, K), F32),
        "z_share": ((32, K), F32),
    }
    return {name: VM(shape, dtype) for name, (shape, dtype) in shapes.items()}


FIRST, COLUMNS, ROWS, LAST = 0, 60, 150, 240
COPIES = 280


def power_kernel(
    row_scale, column_scale, sketch_ref, tiles_ref, byrow_ref, bycol_ref, share_ref, gram_ref, *refs
):
    send, recv = refs[:2]
    ref = dict(zip(scratch_shapes(), refs[2:]))
    row, y = lax.axis_index("rows"), lax.axis_index("cols")
    core = lax.rem(row, 2)
    x = lax.rem(lax.div(row, 2), NX)
    z = lax.div(row, 2 * NX)
    q = lax.rem(row, 2 * NX)

    def at(z_, q_, y_):
        return (z_ * (2 * NX) + q_, y_)

    to_z = lambda p: at(p, q, y)
    to_q = lambda p: at(z, p, y)
    to_x = lambda p: at(z, p * 2 + core, y)
    to_y = lambda p: at(z, q, p)
    other_core = at(z, x * 2 + (1 - core), y)

    barrier = pltpu.get_barrier_semaphore()
    for d in range(1, NZ):
        pl.semaphore_signal(barrier, 1, device_id=to_z(lax.rem(z + d, NZ)), device_id_type=MESH)
    for d in range(1, 2 * NX):
        pl.semaphore_signal(barrier, 1, device_id=to_q(lax.rem(q + d, 2 * NX)), device_id_type=MESH)
    for d in range(1, NY):
        pl.semaphore_signal(barrier, 1, device_id=to_y(lax.rem(y + d, NY)), device_id_type=MESH)
    pl.semaphore_wait(barrier, NZ - 1 + 2 * NX - 1 + NY - 1)

    def gram_of(net, share, parity):
        refs = [ref[name].at[parity] for name in ("g", "g1", "s1", "g2", "s2", "g3", "gf")]
        return gram_sum(net, share, refs, (z, x, core, q, y), to_z, to_q, to_y)

    def half_columns(net, h, value, out):
        xs, part = ref["x_columns" + str(h)], ref["part_columns"].at[h]
        for i, v in enumerate(value):
            xs[y, :, :, i] = v.reshape(2, 2, TILE, W)
        gather = gather4(net, lambda p, i: xs.at[p, i], y, to_y)
        names = ("buf_columns", "tmp_columns", "r0", "c1", "c2", "rz")
        buffers = [ref[name].at[h] for name in names]
        scatter = scatter_rows(net, part, buffers, (z, x, core), to_z, to_x, other_core, out)

        def load(b):
            return xs[b >> 2, (b >> 1) & 1, b & 1].reshape(2 * TILE, W)

        def keep(b, value):
            part[b // 2, b % 2] = value.reshape(2, 2, 32, W)

        def products():
            tile_products(tiles_ref, bycol_ref, load, ref["prefix"], keep, True, True)

        return gather, products, scatter

    def half_rows(net, h, value, out):
        xs = ref[("x_first" if len(value) == 1 else "x_rows") + str(h)]
        part = ref["part_rows"].at[h]
        for i, v in enumerate(value):
            xs[z, lax.div(x, 2), lax.rem(x, 2), core, i] = v
        gather = gather_rows(net, xs, (z, x, core), to_z, to_x, other_core)

        def store(i, value):
            out.append(value.reshape(2 * TILE, W))

        scatter = scatter4(
            net,
            lambda p, i: part.at[p, i],
            y,
            to_y,
            ref["buf_rows"].at[h],
            ref["tmp_rows"].at[h],
            store,
        )

        def load(b):
            both = xs[b >> 1, b & 1]
            parts = [both[:, :, i].reshape(TILE, W) for i in range(both.shape[2])]
            return parts[0] if len(parts) == 1 else jnp.concatenate(parts, axis=0)

        def keep(b, value):
            part[b // 4, (b // 2) % 2, b % 2] = value

        def products():
            tile_products(tiles_ref, byrow_ref, load, ref["prefix"], keep, False, len(value) == 2)

        return gather, products, scatter

    def panel(i):
        factor_panel(i * PANEL, ref["a"], ref["e"], ref["u"], ref["inverse"])

    def factor_begin(scale, parity):
        full = jnp.concatenate([ref["gf"][parity, 0], ref["gf"][parity, 1]], axis=1)
        factor_start(full * scale, ref["a"], ref["e"], ref["u"], ref["inverse"])

    def put(out, share):
        for i, halves in enumerate(zip(*out)):
            value = apply_inverse(jnp.concatenate(halves, axis=1), ref["inverse"][...])
            share[i * value.shape[0] : (i + 1) * value.shape[0], :] = value

    def first():
        net, out = Net(send, recv, FIRST), ([], [])
        g0, p0, s0 = half_rows(net, 0, (sketch_ref[:, :W],), out[0])
        g1, p1, s1 = half_rows(net, 1, (sketch_ref[:, W:],), out[1])
        step(g0, g0, g1, g0, g0)
        p0()
        step(s0, g1, g1, s0, g1)
        p1()
        step(s1, s0, s1, s1)
        for h in range(2):
            for i in range(2):
                ref["y_share"][i * 2 * TILE : (i + 1) * 2 * TILE, h * W : (h + 1) * W] = out[h][i]
        net.drain()

    def columns():
        net, out = Net(send, recv, COLUMNS), ([], [])
        share = ref["y_share"]
        gram = gram_of(net, share[...], 0)
        g0, p0, s0 = half_columns(net, 0, two_parts(share[:, :W]), out[0])
        g1, p1, s1 = half_columns(net, 1, two_parts(share[:, W:]), out[1])
        step(g0, gram, gram, g0, g1, gram, g0)
        p0()
        step(s0, g1, gram, s0, g1)
        p1()
        step(s1, gram, s0, s1, gram)
        factor_begin(row_scale, 0)
        panel(0)
        step(s0, s1)
        panel(1)
        step(s1)
        panel(2)
        panel(3)
        step(s0, s1)
        put(out, ref["z_share"])
        net.drain()

    def rows():
        net, out = Net(send, recv, ROWS), ([], [])
        share = ref["z_share"]
        gram = gram_of(net, share[...], 1)
        g0, p0, s0 = half_rows(net, 0, two_parts(share[:, :W]), out[0])
        g1, p1, s1 = half_rows(net, 1, two_parts(share[:, W:]), out[1])
        step(g0, gram, g0, g1, gram, g0, gram, g0)
        p0()
        step(s0, g1, gram, g1, s0, gram, g1)
        p1()
        step(s1, gram)
        factor_begin(column_scale, 1)
        panel(0)
        panel(1)
        step(s0, s1)
        panel(2)
        panel(3)
        step(s1)
        put(out, ref["y_share"])
        net.drain()

    def one_round(i, carry):
        columns()
        rows()
        return carry

    first()
    lax.fori_loop(0, ROUNDS, one_round, 0)
    net = Net(send, recv, LAST)
    for stage in gram_of(net, ref["y_share"][...], 0):
        pass
    share_ref[...] = ref["y_share"][...]
    gram_ref[:, :128] = ref["gf"][0, 0]
    gram_ref[:, 128:] = ref["gf"][0, 1]
    net.drain()


def power(sketch, tiles, by_row, by_col, row_scale, column_scale):
    vmem, smem = pl.BlockSpec(memory_space=VM), pl.BlockSpec(memory_space=pltpu.SMEM)
    return pl.pallas_call(
        functools.partial(power_kernel, row_scale, column_scale),
        name="power",
        out_shape=(
            jax.ShapeDtypeStruct((4 * TILE, K), F32),
            jax.ShapeDtypeStruct((K, K), F32),
        ),
        in_specs=[vmem, vmem, smem, smem],
        out_specs=[vmem, vmem],
        scratch_shapes=[pltpu.SemaphoreType.DMA((COPIES,))] * 2 + list(scratch_shapes().values()),
        compiler_params=pltpu.CompilerParams(
            collective_id=1, has_side_effects=True, vmem_limit_bytes=48 * MIB
        ),
    )(sketch, tiles, by_row, by_col)


def shards(tiles, tile_rows, tile_cols, tile_counts, sketch):
    row_scale = 1.0 / (TR * TILE * lax.axis_size("rows"))
    column_scale = 1.0 / (CGT * TILE * lax.axis_size("cols"))
    by_row, by_col = slot_orders(tile_rows[0, 0], tile_cols[0, 0], tile_counts[0])
    share, gram = power(sketch[0], tiles[0, 0], by_row, by_col, row_scale, column_scale)
    return factorize(gram, row_scale, share)


def solution(mesh):
    return jax.shard_map(
        shards,
        mesh=mesh,
        in_specs=(
            P("rows", "cols", None, None, None),
            P("rows", "cols", None),
            P("rows", "cols", None),
            P("rows", "cols"),
            P("cols", "rows", None),
        ),
        out_specs=(P(("rows", "cols"), None), P()),
        check_vma=False,
    )
```

```python
import functools

import jax
import jax.numpy as jnp
from jax import lax
from jax.experimental import pallas as pl
from jax.experimental.pallas import tpu as pltpu
from jax.sharding import PartitionSpec as P

ROUNDS = 2
TR = 16
CGT = 16
TILE = 128
K = 256
SLOTS = 32
NZ = 8
NX = 4
NY = 4
PANEL = 64
W = 128
THIN = K // (NX * NY)
F32 = jnp.float32
BF16 = jnp.bfloat16
HI = lax.Precision.HIGHEST
MESH = pl.DeviceIdType.MESH
VM = pltpu.VMEM
MIB = 1024 * 1024


def order_kernel(rows_ref, cols_ref, count_ref, byrow_ref, bycol_ref, cnt_ref):
    live = count_ref[0]

    def one(key_ref, other_ref, out_ref):
        for b in range(TR + 1):
            cnt_ref[b] = 0

        def count(t, carry):
            b = jnp.where(t < live, key_ref[t], TR)
            cnt_ref[b] = cnt_ref[b] + 1
            return carry

        lax.fori_loop(0, SLOTS, count, 0, unroll=True)
        at = jnp.int32(0)
        for b in range(TR + 1):
            n = cnt_ref[b]
            cnt_ref[b] = at
            if b < TR:
                out_ref[112 + b] = jnp.where(n > 0, 1, 0)
                out_ref[96 + b] = jnp.maximum(at + n - 1, 0)
            at = at + n

        def clear(t, carry):
            out_ref[64 + t] = 1
            return carry

        lax.fori_loop(0, SLOTS, clear, 0, unroll=True)
        for b in range(TR + 1):
            first = cnt_ref[b]

            @pl.when(first < SLOTS)
            def _():
                out_ref[64 + first] = 0

        def place(t, carry):
            b = jnp.where(t < live, key_ref[t], TR)
            k = cnt_ref[b]
            cnt_ref[b] = k + 1
            out_ref[k] = t
            out_ref[32 + k] = other_ref[t]
            return carry

        lax.fori_loop(0, SLOTS, place, 0, unroll=True)

    one(rows_ref, cols_ref, byrow_ref)
    one(cols_ref, rows_ref, bycol_ref)


def slot_orders(rows_idx, cols_idx, count):
    smem = pl.BlockSpec(memory_space=pltpu.SMEM)
    out = jax.ShapeDtypeStruct((128,), jnp.int32)
    return pl.pallas_call(
        order_kernel,
        name="orders",
        out_shape=(out, out),
        in_specs=[smem] * 3,
        out_specs=[smem] * 2,
        scratch_shapes=[pltpu.SMEM((TR + 1,), jnp.int32)],
    )(rows_idx, cols_idx, count)


def spread(rows, q):
    return jnp.broadcast_to(rows[q : q + 1, :], (8, 128))


def factor_panel(lo, a_ref, e_ref, u_ref, x_ref):
    groups = PANEL // 8
    first = lo < 128
    a_half = (0, 1) if first else (1,)
    e_half = (0,) if first else (0, 1)
    n_a = len(a_half)
    sub = lax.broadcasted_iota(jnp.int32, (8, 128), 0)

    def rows_of(ref, g, halves):
        return [ref[lo + 8 * g : lo + 8 * g + 8, 128 * h : 128 * h + 128] for h in halves]

    rows = [rows_of(a_ref, g, a_half) + rows_of(e_ref, g, e_half) for g in range(groups)]
    for g in range(groups):
        c = (lo + 8 * g) % 128
        cols = [
            [jnp.broadcast_to(rows[i][0][:, c + q : c + q + 1], (8, 128)) for i in range(g, groups)]
            for q in range(8)
        ]
        done = []
        for q in range(8):
            inv = lax.rsqrt(spread(cols[q][0], q))
            cols[q] = [v * inv for v in cols[q]]
            for p in range(q + 1, 8):
                s = spread(cols[q][0], p)
                cols[p] = [v - w * s for v, w in zip(cols[p], cols[q])]
            row = [spread(v, q) for v in rows[g]]
            for w in range(q):
                s = spread(cols[w][0], q)
                row = [v - s * t for v, t in zip(row, done[w])]
            done.append([v * inv for v in row])
        out = done[0]
        for q in range(1, 8):
            out = [jnp.where(sub == q, v, o) for v, o in zip(done[q], out)]
        at = lo + 8 * g
        for h, v in zip(a_half, out[:n_a]):
            u_ref[at : at + 8, 128 * h : 128 * h + 128] = v
        for h, v in zip(e_half, out[n_a:]):
            x_ref[at : at + 8, 128 * h : 128 * h + 128] = v
        for i in range(g + 1, groups):
            for q in range(8):
                rows[i] = [v - cols[q][i - g] * t for v, t in zip(rows[i], done[q])]
    hi = lo + PANEL
    if hi < K:
        dn = (((0,), (0,)), ((), ()))
        a0 = 0 if hi < 128 else 128
        width = 128 if first else K
        u = u_ref[lo:hi, a0:]
        a_ref[a0:, a0:] -= lax.dot_general(u, u, dn, precision=HI, preferred_element_type=F32)
        e_ref[a0:, :width] -= lax.dot_general(
            u, x_ref[lo:hi, :width], dn, precision=HI, preferred_element_type=F32
        )


def factor_start(gram, a_ref, e_ref, u_ref, x_ref):
    a_ref[...] = gram
    row_i = lax.broadcasted_iota(jnp.int32, (K, K), 0)
    col_i = lax.broadcasted_iota(jnp.int32, (K, K), 1)
    e_ref[...] = jnp.where(row_i == col_i, 1.0, 0.0)
    x_ref[:128, 128:] = jnp.zeros((128, 128), F32)
    u_ref[128:, :128] = jnp.zeros((128, 128), F32)


def factor_kernel(scale, g_ref, y_ref, q_ref, u_ref, x_ref, a_ref, e_ref):
    factor_start(g_ref[...] * scale, a_ref, e_ref, u_ref, x_ref)
    for lo in range(0, K, PANEL):
        factor_panel(lo, a_ref, e_ref, u_ref, x_ref)
    row_i = lax.broadcasted_iota(jnp.int32, (K, K), 0)
    col_i = lax.broadcasted_iota(jnp.int32, (K, K), 1)
    u_ref[...] = jnp.where(col_i >= row_i, u_ref[...], 0.0)
    q_ref[...] = apply_inverse(y_ref[...], x_ref[...])


def apply_inverse(share, inverse):
    return lax.dot_general(
        share, inverse, (((1,), (1,)), ((), ())), precision=HI, preferred_element_type=F32
    )


def factorize(gram, scale, share):
    vmem = pl.BlockSpec(memory_space=VM)
    square = jax.ShapeDtypeStruct((K, K), F32)
    return pl.pallas_call(
        functools.partial(factor_kernel, scale),
        name="factor_apply",
        out_shape=(jax.ShapeDtypeStruct(share.shape, F32), square),
        in_specs=[vmem] * 2,
        out_specs=[vmem] * 2,
        scratch_shapes=[pltpu.VMEM((K, K), F32)] * 3,
        compiler_params=pltpu.CompilerParams(vmem_limit_bytes=32 * MIB),
    )(gram, share)


class Net:
    def __init__(self, send, recv, base):
        self.send, self.recv, self.base, self.copies = send, recv, base, []

    def start(self, src, dst, device):
        k = self.base + len(self.copies)
        copy = pltpu.make_async_remote_copy(
            src_ref=src,
            dst_ref=dst,
            send_sem=self.send.at[k],
            recv_sem=self.recv.at[k],
            device_id=device,
            device_id_type=MESH,
        )
        copy.start()
        self.copies.append(copy)
        return copy

    def drain(self):
        for copy in self.copies:
            copy.wait_send()


def ring4(me):
    return lax.rem(me + 1, 4), lax.rem(me + 3, 4), lax.rem(me + 2, 4)


def gather4(net, loc, me, to, arrived=None):
    arrived = arrived or (lambda p: None)
    right, left, opp = ring4(me)
    r_a = net.start(loc(me, 0), loc(me, 0), to(right))
    l_b = net.start(loc(me, 1), loc(me, 1), to(left))
    r_b = net.start(loc(me, 1), loc(me, 1), to(right))
    l_a = net.start(loc(me, 0), loc(me, 0), to(left))
    arrived(me)
    yield
    r_a.wait_recv()
    f_a = net.start(loc(left, 0), loc(left, 0), to(right))
    l_b.wait_recv()
    f_b = net.start(loc(right, 1), loc(right, 1), to(left))
    yield
    r_b.wait_recv()
    arrived(left)
    l_a.wait_recv()
    arrived(right)
    f_a.wait_recv()
    f_b.wait_recv()
    arrived(opp)


def gather_rows(net, x_ref, where, to_z, to_x, other_core):
    z, x, core = where
    spot = x_ref.at[z, lax.div(x, 2), lax.rem(x, 2), core]
    copies = [net.start(spot, spot, to_z(lax.rem(z + d, NZ))) for d in range(1, NZ)]
    yield
    for copy in copies:
        copy.wait_recv()
    crossing = []

    def cross(p):
        spot = x_ref.at[:, lax.div(p, 2), lax.rem(p, 2), core]
        crossing.append(net.start(spot, spot, other_core))

    def loc(p, h):
        return x_ref.at[pl.ds(h * (NZ // 2), NZ // 2), lax.div(p, 2), lax.rem(p, 2), core]

    yield from gather4(net, loc, x, to_x, cross)
    for copy in crossing:
        copy.wait_recv()


def scatter4(net, src, me, to, buf, tmp, store, ready=None):
    right, left, opp = ring4(me)
    ready = ready or (lambda p: None)
    ready(opp)
    a0 = net.start(src(opp, 0), buf.at[0], to(right))
    b0 = net.start(src(opp, 1), buf.at[1], to(left))
    ready(right)
    b1 = net.start(src(right, 1), buf.at[2], to(right))
    ready(left)
    a1 = net.start(src(left, 0), buf.at[3], to(left))
    yield
    a0.wait_recv()
    tmp[0] = src(right, 0)[...] + buf[0]
    a2 = net.start(tmp.at[0], buf.at[4], to(right))
    b0.wait_recv()
    tmp[1] = src(left, 1)[...] + buf[1]
    b2 = net.start(tmp.at[1], buf.at[5], to(left))
    ready(me)
    yield
    a1.wait_recv()
    b1.wait_recv()
    a2.wait_recv()
    store(0, src(me, 0)[...] + (buf[3] + buf[4]))
    b2.wait_recv()
    store(1, src(me, 1)[...] + (buf[2] + buf[5]))


def scatter_rows(net, part_ref, refs, where, to_z, to_x, other_core, out):
    z, x, core = where
    buf_ref, tmp_ref, r0_ref, c1_ref, c2_ref, rz_ref = refs
    right, left, opp = ring4(x)
    crossing = []
    for p in (opp, right, left, x):
        src = part_ref.at[:, lax.div(p, 2), lax.rem(p, 2), 1 - core]
        crossing.append(net.start(src, r0_ref.at[p], other_core))
    arriving = iter(crossing)
    yield

    def ready(p):
        next(arriving).wait_recv()
        c1_ref[p] = part_ref[:, lax.div(p, 2), lax.rem(p, 2), core] + r0_ref[p]

    def store(h, value):
        c2_ref[pl.ds(h * (NZ // 2), NZ // 2)] = value

    def src(p, h):
        return c1_ref.at[p, pl.ds(h * (NZ // 2), NZ // 2)]

    yield from scatter4(net, src, x, to_x, buf_ref, tmp_ref, store, ready)
    copies = []
    for d in range(1, NZ):
        p = lax.rem(z + d, NZ)
        copies.append(net.start(c2_ref.at[p], rz_ref.at[d - 1], to_z(p)))
    yield
    total = c2_ref[z]
    for d, copy in enumerate(copies):
        copy.wait_recv()
        total = total + rz_ref[d]
    out.append(total)


def gram_sum(net, share, refs, where, to_z, to_xy, other_core):
    g_ref, g0_ref, s0_ref, g1_ref, g2_ref, gf_ref = refs
    z, w, core = where
    gram = lax.dot_general(
        share, share, (((0,), (0,)), ((), ())), precision=HI, preferred_element_type=F32
    )
    g_ref[0] = gram[:, :128]
    g_ref[1] = gram[:, 128:]
    crossing = net.start(g_ref.at[1 - core], g0_ref, other_core)
    yield
    crossing.wait_recv()
    s0_ref[...] = g_ref[core] + g0_ref[...]

    def piece(p):
        return pl.ds(pl.multiple_of(p * THIN, THIN), THIN)

    others = [lax.rem(w + d, NX * NY) for d in range(1, NX * NY)]
    copies = [net.start(s0_ref.at[piece(p)], g1_ref.at[d], to_xy(p)) for d, p in enumerate(others)]
    yield
    total = s0_ref[piece(w)]
    for d, copy in enumerate(copies):
        copy.wait_recv()
        total = total + g1_ref[d]
    g2_ref[z] = total
    spot = g2_ref.at[z]
    copies = [net.start(spot, spot, to_z(lax.rem(z + d, NZ))) for d in range(1, NZ)]
    yield
    for copy in copies:
        copy.wait_recv()
    total = g2_ref[0]
    for d in range(1, NZ):
        total = total + g2_ref[d]
    gf_ref[core, piece(w)] = total
    spot = gf_ref.at[core, piece(w)]
    copies = [net.start(spot, spot, to_xy(p)) for p in others]
    yield
    for copy in copies:
        copy.wait_recv()
    spot = gf_ref.at[core]
    crossing = net.start(spot, spot, other_core)
    yield
    crossing.wait_recv()


def tile_products(tiles_ref, order_ref, load, prefix_ref, store, transposed, twice):
    dn = (((0,), (0,)), ((), ())) if transposed else (((1,), (0,)), ((), ()))

    def step(k, acc):
        tile = tiles_ref[order_ref[k]]
        if twice:
            tile = jnp.concatenate([tile, tile], axis=0 if transposed else 1)
        prod = lax.dot_general(tile, load(order_ref[32 + k]), dn, preferred_element_type=F32)
        acc = acc * order_ref[64 + k].astype(F32) + prod
        prefix_ref[k] = acc
        return acc

    lax.fori_loop(0, SLOTS, step, jnp.zeros((TILE, W), F32), unroll=8)
    for b in range(TR):
        store(b, prefix_ref[order_ref[96 + b]] * order_ref[112 + b].astype(F32))


def two_parts(value):
    high = value.astype(BF16)
    return high, (value - high.astype(F32)).astype(BF16)


def step(*running):
    for stage in running:
        next(stage, None)


def scratch_shapes():
    shapes = {
        "x_first0": ((NZ, 2, 2, 2, 1, 32, W), BF16),
        "x_first1": ((NZ, 2, 2, 2, 1, 32, W), BF16),
        "x_rows0": ((NZ, 2, 2, 2, 2, 32, W), BF16),
        "x_rows1": ((NZ, 2, 2, 2, 2, 32, W), BF16),
        "x_columns0": ((NY, 2, 2, 2, TILE, W), BF16),
        "x_columns1": ((NY, 2, 2, 2, TILE, W), BF16),
        "prefix": ((SLOTS, TILE, W), F32),
        "part_rows": ((2, NY, 2, 2, TILE, W), F32),
        "part_columns": ((2, NZ, 2, 2, 2, 32, W), F32),
        "buf_rows": ((2, 6, 2, TILE, W), F32),
        "tmp_rows": ((2, 2, 2, TILE, W), F32),
        "buf_columns": ((2, 6, NZ // 2, 32, W), F32),
        "tmp_columns": ((2, 2, NZ // 2, 32, W), F32),
        "r0": ((2, NX, NZ, 32, W), F32),
        "c1": ((2, NX, NZ, 32, W), F32),
        "c2": ((2, NZ, 32, W), F32),
        "rz": ((2, NZ - 1, 32, W), F32),
        "g": ((2, 2, K, 128), F32),
        "g0": ((2, K, 128), F32),
        "s0": ((2, K, 128), F32),
        "g1": ((2, NX * NY - 1, THIN, 128), F32),
        "g2": ((2, NZ, THIN, 128), F32),
        "gf": ((2, 2, K, 128), F32),
        "a": ((K, K), F32),
        "e": ((K, K), F32),
        "u": ((K, K), F32),
        "inverse": ((K, K), F32),
        "y_share": ((4 * TILE, K), F32),
        "z_share": ((32, K), F32),
    }
    return {name: VM(shape, dtype) for name, (shape, dtype) in shapes.items()}


FIRST, COLUMNS, ROWS, LAST = 0, 60, 160, 260
COPIES = 310


def power_kernel(
    row_scale, column_scale, sketch_ref, tiles_ref, byrow_ref, bycol_ref, share_ref, gram_ref, *refs
):
    send, recv = refs[:2]
    ref = dict(zip(scratch_shapes(), refs[2:]))
    row, y = lax.axis_index("rows"), lax.axis_index("cols")
    core = lax.rem(row, 2)
    x = lax.rem(lax.div(row, 2), NX)
    z = lax.div(row, 2 * NX)
    q = lax.rem(row, 2 * NX)
    w = x * NY + y

    def at(z_, q_, y_):
        return (z_ * (2 * NX) + q_, y_)

    to_z = lambda p: at(p, q, y)
    to_xy = lambda p: at(z, lax.div(p, NY) * 2 + core, lax.rem(p, NY))
    to_x = lambda p: at(z, p * 2 + core, y)
    to_y = lambda p: at(z, q, p)
    other_core = at(z, x * 2 + (1 - core), y)

    barrier = pltpu.get_barrier_semaphore()
    for d in range(1, NZ):
        pl.semaphore_signal(barrier, 1, device_id=to_z(lax.rem(z + d, NZ)), device_id_type=MESH)
    for d in range(1, NX * NY):
        other = to_xy(lax.rem(w + d, NX * NY))
        pl.semaphore_signal(barrier, 1, device_id=other, device_id_type=MESH)
    pl.semaphore_signal(barrier, 1, device_id=other_core, device_id_type=MESH)
    pl.semaphore_wait(barrier, NZ - 1 + NX * NY - 1 + 1)

    def gram_of(net, share, parity):
        refs = [ref[name].at[parity] for name in ("g", "g0", "s0", "g1", "g2", "gf")]
        return gram_sum(net, share, refs, (z, w, core), to_z, to_xy, other_core)

    def half_columns(net, h, value, out):
        xs, part = ref["x_columns" + str(h)], ref["part_columns"].at[h]
        for i, v in enumerate(value):
            xs[y, :, :, i] = v.reshape(2, 2, TILE, W)
        gather = gather4(net, lambda p, i: xs.at[p, i], y, to_y)
        names = ("buf_columns", "tmp_columns", "r0", "c1", "c2", "rz")
        buffers = [ref[name].at[h] for name in names]
        scatter = scatter_rows(net, part, buffers, (z, x, core), to_z, to_x, other_core, out)

        def load(b):
            return xs[b >> 2, (b >> 1) & 1, b & 1].reshape(2 * TILE, W)

        def keep(b, value):
            part[b // 2, b % 2] = value.reshape(2, 2, 32, W)

        def products():
            tile_products(tiles_ref, bycol_ref, load, ref["prefix"], keep, True, True)

        return gather, products, scatter

    def half_rows(net, h, value, out):
        xs = ref[("x_first" if len(value) == 1 else "x_rows") + str(h)]
        part = ref["part_rows"].at[h]
        for i, v in enumerate(value):
            xs[z, lax.div(x, 2), lax.rem(x, 2), core, i] = v
        gather = gather_rows(net, xs, (z, x, core), to_z, to_x, other_core)

        def store(i, value):
            out.append(value.reshape(2 * TILE, W))

        scatter = scatter4(
            net,
            lambda p, i: part.at[p, i],
            y,
            to_y,
            ref["buf_rows"].at[h],
            ref["tmp_rows"].at[h],
            store,
        )

        def load(b):
            both = xs[b >> 1, b & 1]
            parts = [both[:, :, i].reshape(TILE, W) for i in range(both.shape[2])]
            return parts[0] if len(parts) == 1 else jnp.concatenate(parts, axis=0)

        def keep(b, value):
            part[b // 4, (b // 2) % 2, b % 2] = value

        def products():
            tile_products(tiles_ref, byrow_ref, load, ref["prefix"], keep, False, len(value) == 2)

        return gather, products, scatter

    def panel(i):
        factor_panel(i * PANEL, ref["a"], ref["e"], ref["u"], ref["inverse"])

    def factor_begin(scale, parity):
        full = jnp.concatenate([ref["gf"][parity, 0], ref["gf"][parity, 1]], axis=1)
        factor_start(full * scale, ref["a"], ref["e"], ref["u"], ref["inverse"])

    def put(out, share):
        for i, halves in enumerate(zip(*out)):
            value = apply_inverse(jnp.concatenate(halves, axis=1), ref["inverse"][...])
            share[i * value.shape[0] : (i + 1) * value.shape[0], :] = value

    def first():
        net, out = Net(send, recv, FIRST), ([], [])
        g0, p0, s0 = half_rows(net, 0, (sketch_ref[:, :W],), out[0])
        g1, p1, s1 = half_rows(net, 1, (sketch_ref[:, W:],), out[1])
        step(g0, g0, g1, g0, g0)
        p0()
        step(s0, g1, g1, s0, g1)
        p1()
        step(s1, s0, s1, s1)
        for h in range(2):
            for i in range(2):
                ref["y_share"][i * 2 * TILE : (i + 1) * 2 * TILE, h * W : (h + 1) * W] = out[h][i]
        net.drain()

    def columns():
        net, out = Net(send, recv, COLUMNS), ([], [])
        share = ref["y_share"]
        gram = gram_of(net, share[...], 0)
        g0, p0, s0 = half_columns(net, 0, two_parts(share[:, :W]), out[0])
        g1, p1, s1 = half_columns(net, 1, two_parts(share[:, W:]), out[1])
        step(g0, gram, gram, g0, g1, gram, g0)
        p0()
        step(s0, g1, gram, s0, g1)
        p1()
        step(s1, gram, s0, s1, gram)
        factor_begin(row_scale, 0)
        panel(0)
        step(s0, s1)
        panel(1)
        step(s1)
        panel(2)
        panel(3)
        step(s0, s1)
        put(out, ref["z_share"])
        net.drain()

    def rows():
        net, out = Net(send, recv, ROWS), ([], [])
        share = ref["z_share"]
        gram = gram_of(net, share[...], 1)
        g0, p0, s0 = half_rows(net, 0, two_parts(share[:, :W]), out[0])
        g1, p1, s1 = half_rows(net, 1, two_parts(share[:, W:]), out[1])
        step(g0, gram, g0, g1, gram, g0, gram, g0)
        p0()
        step(s0, g1, gram, g1, s0, gram, g1)
        p1()
        step(s1, gram)
        factor_begin(column_scale, 1)
        panel(0)
        panel(1)
        step(s0, s1)
        panel(2)
        panel(3)
        step(s1)
        put(out, ref["y_share"])
        net.drain()

    def one_round(i, carry):
        columns()
        rows()
        return carry

    first()
    lax.fori_loop(0, ROUNDS, one_round, 0)
    net = Net(send, recv, LAST)
    for stage in gram_of(net, ref["y_share"][...], 0):
        pass
    share_ref[...] = ref["y_share"][...]
    gram_ref[:, :128] = ref["gf"][0, 0]
    gram_ref[:, 128:] = ref["gf"][0, 1]
    net.drain()


def power(sketch, tiles, by_row, by_col, row_scale, column_scale):
    vmem, smem = pl.BlockSpec(memory_space=VM), pl.BlockSpec(memory_space=pltpu.SMEM)
    return pl.pallas_call(
        functools.partial(power_kernel, row_scale, column_scale),
        name="power",
        out_shape=(
            jax.ShapeDtypeStruct((4 * TILE, K), F32),
            jax.ShapeDtypeStruct((K, K), F32),
        ),
        in_specs=[vmem, vmem, smem, smem],
        out_specs=[vmem, vmem],
        scratch_shapes=[pltpu.SemaphoreType.DMA((COPIES,))] * 2 + list(scratch_shapes().values()),
        compiler_params=pltpu.CompilerParams(
            collective_id=1, has_side_effects=True, vmem_limit_bytes=48 * MIB
        ),
    )(sketch, tiles, by_row, by_col)


def shards(tiles, tile_rows, tile_cols, tile_counts, sketch):
    row_scale = 1.0 / (TR * TILE * lax.axis_size("rows"))
    column_scale = 1.0 / (CGT * TILE * lax.axis_size("cols"))
    by_row, by_col = slot_orders(tile_rows[0, 0], tile_cols[0, 0], tile_counts[0])
    share, gram = power(sketch[0], tiles[0, 0], by_row, by_col, row_scale, column_scale)
    return factorize(gram, row_scale, share)


def solution(mesh):
    return jax.shard_map(
        shards,
        mesh=mesh,
        in_specs=(
            P("rows", "cols", None, None, None),
            P("rows", "cols", None),
            P("rows", "cols", None),
            P("rows", "cols"),
            P("cols", "rows", None),
        ),
        out_specs=(P(("rows", "cols"), None), P()),
        check_vma=False,
    )
```

```python
import functools

import jax
import jax.numpy as jnp
from jax import lax
from jax.experimental import pallas as pl
from jax.experimental.pallas import tpu as pltpu
from jax.sharding import PartitionSpec as P

ROUNDS = 2
TR = 16
CGT = 16
TILE = 128
K = 256
SLOTS = 32
NZ = 8
NX = 4
NY = 4
PANEL = 64
W = 128
THIN = K // (NX * NY)
F32 = jnp.float32
BF16 = jnp.bfloat16
HI = lax.Precision.HIGHEST
MESH = pl.DeviceIdType.MESH
VM = pltpu.VMEM
MIB = 1024 * 1024


def order_kernel(rows_ref, cols_ref, count_ref, byrow_ref, bycol_ref, cnt_ref):
    live = count_ref[0]

    def one(key_ref, other_ref, out_ref):
        for b in range(TR + 1):
            cnt_ref[b] = 0

        def count(t, carry):
            b = jnp.where(t < live, key_ref[t], TR)
            cnt_ref[b] = cnt_ref[b] + 1
            return carry

        lax.fori_loop(0, SLOTS, count, 0, unroll=True)
        at = jnp.int32(0)
        for b in range(TR + 1):
            n = cnt_ref[b]
            cnt_ref[b] = at
            if b < TR:
                out_ref[112 + b] = jnp.where(n > 0, 1, 0)
                out_ref[96 + b] = jnp.maximum(at + n - 1, 0)
            at = at + n

        def clear(t, carry):
            out_ref[64 + t] = 1
            return carry

        lax.fori_loop(0, SLOTS, clear, 0, unroll=True)
        for b in range(TR + 1):
            first = cnt_ref[b]

            @pl.when(first < SLOTS)
            def _():
                out_ref[64 + first] = 0

        def place(t, carry):
            b = jnp.where(t < live, key_ref[t], TR)
            k = cnt_ref[b]
            cnt_ref[b] = k + 1
            out_ref[k] = t
            out_ref[32 + k] = other_ref[t]
            return carry

        lax.fori_loop(0, SLOTS, place, 0, unroll=True)

    one(rows_ref, cols_ref, byrow_ref)
    one(cols_ref, rows_ref, bycol_ref)


def slot_orders(rows_idx, cols_idx, count):
    smem = pl.BlockSpec(memory_space=pltpu.SMEM)
    out = jax.ShapeDtypeStruct((128,), jnp.int32)
    return pl.pallas_call(
        order_kernel,
        name="orders",
        out_shape=(out, out),
        in_specs=[smem] * 3,
        out_specs=[smem] * 2,
        scratch_shapes=[pltpu.SMEM((TR + 1,), jnp.int32)],
    )(rows_idx, cols_idx, count)


def spread(rows, q):
    return jnp.broadcast_to(rows[q : q + 1, :], (8, 128))


def factor_panel(lo, a_ref, e_ref, u_ref, x_ref):
    groups = PANEL // 8
    first = lo < 128
    a_half = (0, 1) if first else (1,)
    e_half = (0,) if first else (0, 1)
    n_a = len(a_half)
    sub = lax.broadcasted_iota(jnp.int32, (8, 128), 0)

    def rows_of(ref, g, halves):
        return [ref[lo + 8 * g : lo + 8 * g + 8, 128 * h : 128 * h + 128] for h in halves]

    rows = [rows_of(a_ref, g, a_half) + rows_of(e_ref, g, e_half) for g in range(groups)]
    for g in range(groups):
        c = (lo + 8 * g) % 128
        cols = [
            [jnp.broadcast_to(rows[i][0][:, c + q : c + q + 1], (8, 128)) for i in range(g, groups)]
            for q in range(8)
        ]
        done = []
        for q in range(8):
            inv = lax.rsqrt(spread(cols[q][0], q))
            cols[q] = [v * inv for v in cols[q]]
            for p in range(q + 1, 8):
                s = spread(cols[q][0], p)
                cols[p] = [v - w * s for v, w in zip(cols[p], cols[q])]
            row = [spread(v, q) for v in rows[g]]
            for w in range(q):
                s = spread(cols[w][0], q)
                row = [v - s * t for v, t in zip(row, done[w])]
            done.append([v * inv for v in row])
        out = done[0]
        for q in range(1, 8):
            out = [jnp.where(sub == q, v, o) for v, o in zip(done[q], out)]
        at = lo + 8 * g
        for h, v in zip(a_half, out[:n_a]):
            u_ref[at : at + 8, 128 * h : 128 * h + 128] = v
        for h, v in zip(e_half, out[n_a:]):
            x_ref[at : at + 8, 128 * h : 128 * h + 128] = v
        for i in range(g + 1, groups):
            for q in range(8):
                rows[i] = [v - cols[q][i - g] * t for v, t in zip(rows[i], done[q])]
    hi = lo + PANEL
    if hi < K:
        dn = (((0,), (0,)), ((), ()))
        a0 = 0 if hi < 128 else 128
        width = 128 if first else K
        u = u_ref[lo:hi, a0:]
        a_ref[a0:, a0:] -= lax.dot_general(u, u, dn, precision=HI, preferred_element_type=F32)
        e_ref[a0:, :width] -= lax.dot_general(
            u, x_ref[lo:hi, :width], dn, precision=HI, preferred_element_type=F32
        )


def factor_start(gram, a_ref, e_ref, u_ref, x_ref):
    a_ref[...] = gram
    row_i = lax.broadcasted_iota(jnp.int32, (K, K), 0)
    col_i = lax.broadcasted_iota(jnp.int32, (K, K), 1)
    e_ref[...] = jnp.where(row_i == col_i, 1.0, 0.0)
    x_ref[:128, 128:] = jnp.zeros((128, 128), F32)
    u_ref[128:, :128] = jnp.zeros((128, 128), F32)


def factor_kernel(scale, g_ref, y_ref, q_ref, u_ref, x_ref, a_ref, e_ref):
    factor_start(g_ref[...] * scale, a_ref, e_ref, u_ref, x_ref)
    for lo in range(0, K, PANEL):
        factor_panel(lo, a_ref, e_ref, u_ref, x_ref)
    row_i = lax.broadcasted_iota(jnp.int32, (K, K), 0)
    col_i = lax.broadcasted_iota(jnp.int32, (K, K), 1)
    u_ref[...] = jnp.where(col_i >= row_i, u_ref[...], 0.0)
    q_ref[...] = apply_inverse(y_ref[...], x_ref[...])


def apply_inverse(share, inverse):
    return lax.dot_general(
        share, inverse, (((1,), (1,)), ((), ())), precision=HI, preferred_element_type=F32
    )


def factorize(gram, scale, share):
    vmem = pl.BlockSpec(memory_space=VM)
    square = jax.ShapeDtypeStruct((K, K), F32)
    return pl.pallas_call(
        functools.partial(factor_kernel, scale),
        name="factor_apply",
        out_shape=(jax.ShapeDtypeStruct(share.shape, F32), square),
        in_specs=[vmem] * 2,
        out_specs=[vmem] * 2,
        scratch_shapes=[pltpu.VMEM((K, K), F32)] * 3,
        compiler_params=pltpu.CompilerParams(vmem_limit_bytes=32 * MIB),
    )(gram, share)


class Net:
    def __init__(self, send, recv, base):
        self.send, self.recv, self.base, self.copies = send, recv, base, []

    def start(self, src, dst, device):
        k = self.base + len(self.copies)
        copy = pltpu.make_async_remote_copy(
            src_ref=src,
            dst_ref=dst,
            send_sem=self.send.at[k],
            recv_sem=self.recv.at[k],
            device_id=device,
            device_id_type=MESH,
        )
        copy.start()
        self.copies.append(copy)
        return copy

    def drain(self):
        for copy in self.copies:
            copy.wait_send()


def ring4(me):
    return lax.rem(me + 1, 4), lax.rem(me + 3, 4), lax.rem(me + 2, 4)


def gather4(net, loc, me, to, arrived=None):
    arrived = arrived or (lambda p: None)
    right, left, opp = ring4(me)
    r_a = net.start(loc(me, 0), loc(me, 0), to(right))
    l_b = net.start(loc(me, 1), loc(me, 1), to(left))
    r_b = net.start(loc(me, 1), loc(me, 1), to(right))
    l_a = net.start(loc(me, 0), loc(me, 0), to(left))
    arrived(me)
    yield
    r_a.wait_recv()
    f_a = net.start(loc(left, 0), loc(left, 0), to(right))
    l_b.wait_recv()
    f_b = net.start(loc(right, 1), loc(right, 1), to(left))
    yield
    r_b.wait_recv()
    arrived(left)
    l_a.wait_recv()
    arrived(right)
    f_a.wait_recv()
    f_b.wait_recv()
    arrived(opp)


def gather_rows(net, x_ref, where, to_z, to_x, other_core):
    z, x, core = where
    spot = x_ref.at[z, lax.div(x, 2), lax.rem(x, 2), core]
    copies = [net.start(spot, spot, to_z(lax.rem(z + d, NZ))) for d in range(1, NZ)]
    yield
    for copy in copies:
        copy.wait_recv()
    crossing = []

    def cross(p):
        spot = x_ref.at[:, lax.div(p, 2), lax.rem(p, 2), core]
        crossing.append(net.start(spot, spot, other_core))

    def loc(p, h):
        return x_ref.at[pl.ds(h * (NZ // 2), NZ // 2), lax.div(p, 2), lax.rem(p, 2), core]

    yield from gather4(net, loc, x, to_x, cross)
    for copy in crossing:
        copy.wait_recv()


def scatter4(net, src, me, to, buf, tmp, store, ready=None):
    right, left, opp = ring4(me)
    ready = ready or (lambda p: None)
    ready(opp)
    a0 = net.start(src(opp, 0), buf.at[0], to(right))
    b0 = net.start(src(opp, 1), buf.at[1], to(left))
    ready(right)
    b1 = net.start(src(right, 1), buf.at[2], to(right))
    ready(left)
    a1 = net.start(src(left, 0), buf.at[3], to(left))
    yield
    a0.wait_recv()
    tmp[0] = src(right, 0)[...] + buf[0]
    a2 = net.start(tmp.at[0], buf.at[4], to(right))
    b0.wait_recv()
    tmp[1] = src(left, 1)[...] + buf[1]
    b2 = net.start(tmp.at[1], buf.at[5], to(left))
    ready(me)
    yield
    a1.wait_recv()
    b1.wait_recv()
    a2.wait_recv()
    store(0, src(me, 0)[...] + (buf[3] + buf[4]))
    b2.wait_recv()
    store(1, src(me, 1)[...] + (buf[2] + buf[5]))


def scatter_rows(net, part_ref, refs, where, to_z, to_x, other_core, out):
    z, x, core = where
    buf_ref, tmp_ref, r0_ref, c1_ref, c2_ref, rz_ref = refs
    right, left, opp = ring4(x)
    crossing = []
    for p in (opp, right, left, x):
        src = part_ref.at[:, lax.div(p, 2), lax.rem(p, 2), 1 - core]
        crossing.append(net.start(src, r0_ref.at[p], other_core))
    arriving = iter(crossing)
    yield

    def ready(p):
        next(arriving).wait_recv()
        c1_ref[p] = part_ref[:, lax.div(p, 2), lax.rem(p, 2), core] + r0_ref[p]

    def store(h, value):
        c2_ref[pl.ds(h * (NZ // 2), NZ // 2)] = value

    def src(p, h):
        return c1_ref.at[p, pl.ds(h * (NZ // 2), NZ // 2)]

    yield from scatter4(net, src, x, to_x, buf_ref, tmp_ref, store, ready)
    copies = []
    for d in range(1, NZ):
        p = lax.rem(z + d, NZ)
        copies.append(net.start(c2_ref.at[p], rz_ref.at[d - 1], to_z(p)))
    yield
    total = c2_ref[z]
    for d, copy in enumerate(copies):
        copy.wait_recv()
        total = total + rz_ref[d]
    out.append(total)


def gram_sum(net, share, refs, where, to_z, to_xy, other_core):
    g_ref, g0_ref, s0_ref, g1_ref, g2_ref, gf_ref = refs
    z, w, core = where
    gram = lax.dot_general(
        share, share, (((0,), (0,)), ((), ())), precision=HI, preferred_element_type=F32
    )
    g_ref[0] = gram[:, :128]
    g_ref[1] = gram[:, 128:]
    crossing = net.start(g_ref.at[1 - core], g0_ref, other_core)
    yield
    crossing.wait_recv()
    s0_ref[...] = g_ref[core] + g0_ref[...]

    def piece(p):
        return pl.ds(pl.multiple_of(p * THIN, THIN), THIN)

    others = [lax.rem(w + d, NX * NY) for d in range(1, NX * NY)]
    copies = [net.start(s0_ref.at[piece(p)], g1_ref.at[d], to_xy(p)) for d, p in enumerate(others)]
    yield
    total = s0_ref[piece(w)]
    for d, copy in enumerate(copies):
        copy.wait_recv()
        total = total + g1_ref[d]
    g2_ref[z] = total
    spot = g2_ref.at[z]
    copies = [net.start(spot, spot, to_z(lax.rem(z + d, NZ))) for d in range(1, NZ)]
    yield
    for copy in copies:
        copy.wait_recv()
    total = g2_ref[0]
    for d in range(1, NZ):
        total = total + g2_ref[d]
    gf_ref[core, piece(w)] = total
    spot = gf_ref.at[core, piece(w)]
    copies = [net.start(spot, spot, to_xy(p)) for p in others]
    yield
    for copy in copies:
        copy.wait_recv()
    spot = gf_ref.at[core]
    crossing = net.start(spot, spot, other_core)
    yield
    crossing.wait_recv()


def tile_products(tiles_ref, order_ref, load, prefix_ref, store, transposed, twice):
    dn = (((0,), (0,)), ((), ())) if transposed else (((1,), (0,)), ((), ()))

    def step(k, acc):
        tile = tiles_ref[order_ref[k]]
        if twice:
            tile = jnp.concatenate([tile, tile], axis=0 if transposed else 1)
        prod = lax.dot_general(tile, load(order_ref[32 + k]), dn, preferred_element_type=F32)
        acc = acc * order_ref[64 + k].astype(F32) + prod
        prefix_ref[k] = acc
        return acc

    lax.fori_loop(0, SLOTS, step, jnp.zeros((TILE, W), F32), unroll=8)
    for b in range(TR):
        store(b, prefix_ref[order_ref[96 + b]] * order_ref[112 + b].astype(F32))


def two_parts(value):
    high = value.astype(BF16)
    return high, (value - high.astype(F32)).astype(BF16)


def step(*running):
    for stage in running:
        next(stage, None)


def scratch_shapes():
    shapes = {
        "x_first0": ((NZ, 2, 2, 2, 1, 32, W), BF16),
        "x_first1": ((NZ, 2, 2, 2, 1, 32, W), BF16),
        "x_rows0": ((NZ, 2, 2, 2, 2, 32, W), BF16),
        "x_rows1": ((NZ, 2, 2, 2, 2, 32, W), BF16),
        "x_columns0": ((NY, 2, 2, 2, TILE, W), BF16),
        "x_columns1": ((NY, 2, 2, 2, TILE, W), BF16),
        "tiles": ((SLOTS, TILE, TILE), BF16),
        "prefix": ((SLOTS, TILE, W), F32),
        "part_rows": ((2, NY, 2, 2, TILE, W), F32),
        "part_columns": ((2, NZ, 2, 2, 2, 32, W), F32),
        "buf_rows": ((2, 6, 2, TILE, W), F32),
        "tmp_rows": ((2, 2, 2, TILE, W), F32),
        "buf_columns": ((2, 6, NZ // 2, 32, W), F32),
        "tmp_columns": ((2, 2, NZ // 2, 32, W), F32),
        "r0": ((2, NX, NZ, 32, W), F32),
        "c1": ((2, NX, NZ, 32, W), F32),
        "c2": ((2, NZ, 32, W), F32),
        "rz": ((2, NZ - 1, 32, W), F32),
        "g": ((2, 2, K, 128), F32),
        "g0": ((2, K, 128), F32),
        "s0": ((2, K, 128), F32),
        "g1": ((2, NX * NY - 1, THIN, 128), F32),
        "g2": ((2, NZ, THIN, 128), F32),
        "gf": ((2, 2, K, 128), F32),
        "a": ((K, K), F32),
        "e": ((K, K), F32),
        "u": ((K, K), F32),
        "inverse": ((K, K), F32),
        "y_share": ((4 * TILE, K), F32),
        "z_share": ((32, K), F32),
    }
    return {name: VM(shape, dtype) for name, (shape, dtype) in shapes.items()}


FIRST, COLUMNS, ROWS, LAST = 0, 60, 160, 260
COPIES = 310


def power_kernel(
    row_scale, column_scale, sketch_ref, stored_ref, byrow_ref, bycol_ref, share_ref, gram_ref, *refs
):
    send, recv, tiles_sem = refs[:3]
    ref = dict(zip(scratch_shapes(), refs[3:]))
    tiles_ref = ref["tiles"]
    fetch = pltpu.make_async_copy(stored_ref, tiles_ref, tiles_sem)
    fetch.start()
    row, y = lax.axis_index("rows"), lax.axis_index("cols")
    core = lax.rem(row, 2)
    x = lax.rem(lax.div(row, 2), NX)
    z = lax.div(row, 2 * NX)
    q = lax.rem(row, 2 * NX)
    w = x * NY + y

    def at(z_, q_, y_):
        return (z_ * (2 * NX) + q_, y_)

    to_z = lambda p: at(p, q, y)
    to_xy = lambda p: at(z, lax.div(p, NY) * 2 + core, lax.rem(p, NY))
    to_x = lambda p: at(z, p * 2 + core, y)
    to_y = lambda p: at(z, q, p)
    other_core = at(z, x * 2 + (1 - core), y)

    barrier = pltpu.get_barrier_semaphore()
    for d in range(1, NZ):
        pl.semaphore_signal(barrier, 1, device_id=to_z(lax.rem(z + d, NZ)), device_id_type=MESH)
    for d in range(1, NX * NY):
        other = to_xy(lax.rem(w + d, NX * NY))
        pl.semaphore_signal(barrier, 1, device_id=other, device_id_type=MESH)
    pl.semaphore_signal(barrier, 1, device_id=other_core, device_id_type=MESH)
    pl.semaphore_wait(barrier, NZ - 1 + NX * NY - 1 + 1)

    def gram_of(net, share, parity):
        refs = [ref[name].at[parity] for name in ("g", "g0", "s0", "g1", "g2", "gf")]
        return gram_sum(net, share, refs, (z, w, core), to_z, to_xy, other_core)

    def half_columns(net, h, value, out):
        xs, part = ref["x_columns" + str(h)], ref["part_columns"].at[h]
        for i, v in enumerate(value):
            xs[y, :, :, i] = v.reshape(2, 2, TILE, W)
        gather = gather4(net, lambda p, i: xs.at[p, i], y, to_y)
        names = ("buf_columns", "tmp_columns", "r0", "c1", "c2", "rz")
        buffers = [ref[name].at[h] for name in names]
        scatter = scatter_rows(net, part, buffers, (z, x, core), to_z, to_x, other_core, out)

        def load(b):
            return xs[b >> 2, (b >> 1) & 1, b & 1].reshape(2 * TILE, W)

        def keep(b, value):
            part[b // 2, b % 2] = value.reshape(2, 2, 32, W)

        def products():
            tile_products(tiles_ref, bycol_ref, load, ref["prefix"], keep, True, True)

        return gather, products, scatter

    def half_rows(net, h, value, out):
        xs = ref[("x_first" if len(value) == 1 else "x_rows") + str(h)]
        part = ref["part_rows"].at[h]
        for i, v in enumerate(value):
            xs[z, lax.div(x, 2), lax.rem(x, 2), core, i] = v
        gather = gather_rows(net, xs, (z, x, core), to_z, to_x, other_core)

        def store(i, value):
            out.append(value.reshape(2 * TILE, W))

        scatter = scatter4(
            net,
            lambda p, i: part.at[p, i],
            y,
            to_y,
            ref["buf_rows"].at[h],
            ref["tmp_rows"].at[h],
            store,
        )

        def load(b):
            both = xs[b >> 1, b & 1]
            parts = [both[:, :, i].reshape(TILE, W) for i in range(both.shape[2])]
            return parts[0] if len(parts) == 1 else jnp.concatenate(parts, axis=0)

        def keep(b, value):
            part[b // 4, (b // 2) % 2, b % 2] = value

        def products():
            tile_products(tiles_ref, byrow_ref, load, ref["prefix"], keep, False, len(value) == 2)

        return gather, products, scatter

    def panel(i):
        factor_panel(i * PANEL, ref["a"], ref["e"], ref["u"], ref["inverse"])

    def factor_begin(scale, parity):
        full = jnp.concatenate([ref["gf"][parity, 0], ref["gf"][parity, 1]], axis=1)
        factor_start(full * scale, ref["a"], ref["e"], ref["u"], ref["inverse"])

    def put(out, share):
        for i, halves in enumerate(zip(*out)):
            value = apply_inverse(jnp.concatenate(halves, axis=1), ref["inverse"][...])
            share[i * value.shape[0] : (i + 1) * value.shape[0], :] = value

    def first():
        net, out = Net(send, recv, FIRST), ([], [])
        g0, p0, s0 = half_rows(net, 0, (sketch_ref[:, :W],), out[0])
        g1, p1, s1 = half_rows(net, 1, (sketch_ref[:, W:],), out[1])
        step(g0, g0, g1, g0, g0)
        fetch.wait()
        p0()
        step(s0, g1, g1, s0, g1)
        p1()
        step(s1, s0, s1, s1)
        for h in range(2):
            for i in range(2):
                ref["y_share"][i * 2 * TILE : (i + 1) * 2 * TILE, h * W : (h + 1) * W] = out[h][i]
        net.drain()

    def columns():
        net, out = Net(send, recv, COLUMNS), ([], [])
        share = ref["y_share"]
        gram = gram_of(net, share[...], 0)
        g0, p0, s0 = half_columns(net, 0, two_parts(share[:, :W]), out[0])
        g1, p1, s1 = half_columns(net, 1, two_parts(share[:, W:]), out[1])
        step(g0, gram, gram, g0, g1, gram, g0)
        p0()
        step(s0, g1, gram, s0, g1)
        p1()
        step(s1, gram, s0, s1, gram)
        factor_begin(row_scale, 0)
        panel(0)
        step(s0, s1)
        panel(1)
        step(s1)
        panel(2)
        panel(3)
        step(s0, s1)
        put(out, ref["z_share"])
        net.drain()

    def rows():
        net, out = Net(send, recv, ROWS), ([], [])
        share = ref["z_share"]
        gram = gram_of(net, share[...], 1)
        g0, p0, s0 = half_rows(net, 0, two_parts(share[:, :W]), out[0])
        g1, p1, s1 = half_rows(net, 1, two_parts(share[:, W:]), out[1])
        step(g0, gram, g0, g1, gram, g0, gram, g0)
        p0()
        step(s0, g1, gram, g1, s0, gram, g1)
        p1()
        step(s1, gram)
        factor_begin(column_scale, 1)
        panel(0)
        panel(1)
        step(s0, s1)
        panel(2)
        panel(3)
        step(s1)
        put(out, ref["y_share"])
        net.drain()

    def one_round(i, carry):
        columns()
        rows()
        return carry

    first()
    lax.fori_loop(0, ROUNDS, one_round, 0)
    net = Net(send, recv, LAST)
    for stage in gram_of(net, ref["y_share"][...], 0):
        pass
    share_ref[...] = ref["y_share"][...]
    gram_ref[:, :128] = ref["gf"][0, 0]
    gram_ref[:, 128:] = ref["gf"][0, 1]
    net.drain()


def power(sketch, tiles, by_row, by_col, row_scale, column_scale):
    vmem, smem = pl.BlockSpec(memory_space=VM), pl.BlockSpec(memory_space=pltpu.SMEM)
    return pl.pallas_call(
        functools.partial(power_kernel, row_scale, column_scale),
        name="power",
        out_shape=(
            jax.ShapeDtypeStruct((4 * TILE, K), F32),
            jax.ShapeDtypeStruct((K, K), F32),
        ),
        in_specs=[vmem, pl.BlockSpec(memory_space=pl.ANY), smem, smem],
        out_specs=[vmem, vmem],
        scratch_shapes=[pltpu.SemaphoreType.DMA((COPIES,))] * 2
        + [pltpu.SemaphoreType.DMA]
        + list(scratch_shapes().values()),
        compiler_params=pltpu.CompilerParams(
            collective_id=1, has_side_effects=True, vmem_limit_bytes=48 * MIB
        ),
    )(sketch, tiles, by_row, by_col)


def shards(tiles, tile_rows, tile_cols, tile_counts, sketch):
    row_scale = 1.0 / (TR * TILE * lax.axis_size("rows"))
    column_scale = 1.0 / (CGT * TILE * lax.axis_size("cols"))
    by_row, by_col = slot_orders(tile_rows[0, 0], tile_cols[0, 0], tile_counts[0])
    share, gram = power(sketch[0], tiles[0, 0], by_row, by_col, row_scale, column_scale)
    return factorize(gram, row_scale, share)


def solution(mesh):
    return jax.shard_map(
        shards,
        mesh=mesh,
        in_specs=(
            P("rows", "cols", None, None, None),
            P("rows", "cols", None),
            P("rows", "cols", None),
            P("rows", "cols"),
            P("cols", "rows", None),
        ),
        out_specs=(P(("rows", "cols"), None), P()),
        check_vma=False,
    )
```

```python
import functools

import jax
import jax.numpy as jnp
from jax import lax
from jax.experimental import pallas as pl
from jax.experimental.pallas import tpu as pltpu
from jax.sharding import PartitionSpec as P

ROUNDS = 2
TR = 16
CGT = 16
TILE = 128
K = 256
SLOTS = 32
NZ = 8
NX = 4
NY = 4
PANEL = 64
W = 128
THIN = K // (NX * NY)
F32 = jnp.float32
BF16 = jnp.bfloat16
HI = lax.Precision.HIGHEST
MESH = pl.DeviceIdType.MESH
VM = pltpu.VMEM
MIB = 1024 * 1024


def order_kernel(rows_ref, cols_ref, count_ref, byrow_ref, bycol_ref, cnt_ref):
    live = count_ref[0]

    def one(key_ref, other_ref, out_ref):
        for b in range(TR + 1):
            cnt_ref[b] = 0

        def count(t, carry):
            b = jnp.where(t < live, key_ref[t], TR)
            cnt_ref[b] = cnt_ref[b] + 1
            return carry

        lax.fori_loop(0, SLOTS, count, 0, unroll=True)
        at = jnp.int32(0)
        for b in range(TR + 1):
            n = cnt_ref[b]
            cnt_ref[b] = at
            if b < TR:
                out_ref[112 + b] = jnp.where(n > 0, 1, 0)
                out_ref[96 + b] = jnp.maximum(at + n - 1, 0)
            at = at + n

        def clear(t, carry):
            out_ref[64 + t] = 1
            return carry

        lax.fori_loop(0, SLOTS, clear, 0, unroll=True)
        for b in range(TR + 1):
            first = cnt_ref[b]

            @pl.when(first < SLOTS)
            def _():
                out_ref[64 + first] = 0

        def place(t, carry):
            b = jnp.where(t < live, key_ref[t], TR)
            k = cnt_ref[b]
            cnt_ref[b] = k + 1
            out_ref[k] = t
            out_ref[32 + k] = other_ref[t]
            return carry

        lax.fori_loop(0, SLOTS, place, 0, unroll=True)

    one(rows_ref, cols_ref, byrow_ref)
    one(cols_ref, rows_ref, bycol_ref)


def slot_orders(rows_idx, cols_idx, count):
    smem = pl.BlockSpec(memory_space=pltpu.SMEM)
    out = jax.ShapeDtypeStruct((128,), jnp.int32)
    return pl.pallas_call(
        order_kernel,
        name="orders",
        out_shape=(out, out),
        in_specs=[smem] * 3,
        out_specs=[smem] * 2,
        scratch_shapes=[pltpu.SMEM((TR + 1,), jnp.int32)],
    )(rows_idx, cols_idx, count)


def spread(rows, q):
    return jnp.broadcast_to(rows[q : q + 1, :], (8, 128))


def factor_panel(lo, a_ref, e_ref, u_ref, x_ref):
    groups = PANEL // 8
    first = lo < 128
    a_half = (0, 1) if first else (1,)
    e_half = (0,) if first else (0, 1)
    n_a = len(a_half)
    sub = lax.broadcasted_iota(jnp.int32, (8, 128), 0)

    def rows_of(ref, g, halves):
        return [ref[lo + 8 * g : lo + 8 * g + 8, 128 * h : 128 * h + 128] for h in halves]

    rows = [rows_of(a_ref, g, a_half) + rows_of(e_ref, g, e_half) for g in range(groups)]
    for g in range(groups):
        c = (lo + 8 * g) % 128
        cols = [
            [jnp.broadcast_to(rows[i][0][:, c + q : c + q + 1], (8, 128)) for i in range(g, groups)]
            for q in range(8)
        ]
        done = []
        for q in range(8):
            inv = lax.rsqrt(spread(cols[q][0], q))
            cols[q] = [v * inv for v in cols[q]]
            for p in range(q + 1, 8):
                s = spread(cols[q][0], p)
                cols[p] = [v - w * s for v, w in zip(cols[p], cols[q])]
            row = [spread(v, q) for v in rows[g]]
            for w in range(q):
                s = spread(cols[w][0], q)
                row = [v - s * t for v, t in zip(row, done[w])]
            done.append([v * inv for v in row])
        out = done[0]
        for q in range(1, 8):
            out = [jnp.where(sub == q, v, o) for v, o in zip(done[q], out)]
        at = lo + 8 * g
        for h, v in zip(a_half, out[:n_a]):
            u_ref[at : at + 8, 128 * h : 128 * h + 128] = v
        for h, v in zip(e_half, out[n_a:]):
            x_ref[at : at + 8, 128 * h : 128 * h + 128] = v
        for i in range(g + 1, groups):
            for q in range(8):
                rows[i] = [v - cols[q][i - g] * t for v, t in zip(rows[i], done[q])]
    hi = lo + PANEL
    if hi < K:
        dn = (((0,), (0,)), ((), ()))
        a0 = 0 if hi < 128 else 128
        width = 128 if first else K
        u = u_ref[lo:hi, a0:]
        a_ref[a0:, a0:] -= lax.dot_general(u, u, dn, precision=HI, preferred_element_type=F32)
        e_ref[a0:, :width] -= lax.dot_general(
            u, x_ref[lo:hi, :width], dn, precision=HI, preferred_element_type=F32
        )


def factor_start(gram, a_ref, e_ref, u_ref, x_ref):
    a_ref[...] = gram
    row_i = lax.broadcasted_iota(jnp.int32, (K, K), 0)
    col_i = lax.broadcasted_iota(jnp.int32, (K, K), 1)
    e_ref[...] = jnp.where(row_i == col_i, 1.0, 0.0)
    x_ref[:128, 128:] = jnp.zeros((128, 128), F32)
    u_ref[128:, :128] = jnp.zeros((128, 128), F32)


def factor_kernel(scale, g_ref, y_ref, q_ref, u_ref, x_ref, a_ref, e_ref):
    factor_start(g_ref[...] * scale, a_ref, e_ref, u_ref, x_ref)
    for lo in range(0, K, PANEL):
        factor_panel(lo, a_ref, e_ref, u_ref, x_ref)
    row_i = lax.broadcasted_iota(jnp.int32, (K, K), 0)
    col_i = lax.broadcasted_iota(jnp.int32, (K, K), 1)
    u_ref[...] = jnp.where(col_i >= row_i, u_ref[...], 0.0)
    q_ref[...] = apply_inverse(y_ref[...], x_ref[...])


def apply_inverse(share, inverse):
    return lax.dot_general(
        share, inverse, (((1,), (1,)), ((), ())), precision=HI, preferred_element_type=F32
    )


def factorize(gram, scale, share):
    vmem = pl.BlockSpec(memory_space=VM)
    square = jax.ShapeDtypeStruct((K, K), F32)
    return pl.pallas_call(
        functools.partial(factor_kernel, scale),
        name="factor_apply",
        out_shape=(jax.ShapeDtypeStruct(share.shape, F32), square),
        in_specs=[vmem] * 2,
        out_specs=[vmem] * 2,
        scratch_shapes=[pltpu.VMEM((K, K), F32)] * 3,
        compiler_params=pltpu.CompilerParams(vmem_limit_bytes=32 * MIB),
    )(gram, share)


class Net:
    def __init__(self, send, recv, base):
        self.send, self.recv, self.base, self.copies = send, recv, base, []

    def start(self, src, dst, device):
        k = self.base + len(self.copies)
        copy = pltpu.make_async_remote_copy(
            src_ref=src,
            dst_ref=dst,
            send_sem=self.send.at[k],
            recv_sem=self.recv.at[k],
            device_id=device,
            device_id_type=MESH,
        )
        copy.start()
        self.copies.append(copy)
        return copy

    def drain(self):
        for copy in self.copies:
            copy.wait_send()


def ring4(me):
    return lax.rem(me + 1, 4), lax.rem(me + 3, 4), lax.rem(me + 2, 4)


def gather4(net, loc, me, to, arrived=None):
    arrived = arrived or (lambda p: None)
    right, left, opp = ring4(me)
    r_a = net.start(loc(me, 0), loc(me, 0), to(right))
    l_b = net.start(loc(me, 1), loc(me, 1), to(left))
    r_b = net.start(loc(me, 1), loc(me, 1), to(right))
    l_a = net.start(loc(me, 0), loc(me, 0), to(left))
    arrived(me)
    yield
    r_a.wait_recv()
    f_a = net.start(loc(left, 0), loc(left, 0), to(right))
    l_b.wait_recv()
    f_b = net.start(loc(right, 1), loc(right, 1), to(left))
    yield
    r_b.wait_recv()
    arrived(left)
    l_a.wait_recv()
    arrived(right)
    f_a.wait_recv()
    f_b.wait_recv()
    arrived(opp)


def gather_rows(net, x_ref, where, to_z, to_x, other_core):
    z, x, core = where
    spot = x_ref.at[z, lax.div(x, 2), lax.rem(x, 2), core]
    copies = [net.start(spot, spot, to_z(lax.rem(z + d, NZ))) for d in range(1, NZ)]
    yield
    for copy in copies:
        copy.wait_recv()
    crossing = []

    def cross(p):
        spot = x_ref.at[:, lax.div(p, 2), lax.rem(p, 2), core]
        crossing.append(net.start(spot, spot, other_core))

    def loc(p, h):
        return x_ref.at[pl.ds(h * (NZ // 2), NZ // 2), lax.div(p, 2), lax.rem(p, 2), core]

    yield from gather4(net, loc, x, to_x, cross)
    for copy in crossing:
        copy.wait_recv()


def scatter4(net, src, me, to, buf, tmp, store, ready=None):
    right, left, opp = ring4(me)
    ready = ready or (lambda p: None)
    ready(opp)
    a0 = net.start(src(opp, 0), buf.at[0], to(right))
    b0 = net.start(src(opp, 1), buf.at[1], to(left))
    ready(right)
    b1 = net.start(src(right, 1), buf.at[2], to(right))
    ready(left)
    a1 = net.start(src(left, 0), buf.at[3], to(left))
    yield
    a0.wait_recv()
    tmp[0] = src(right, 0)[...] + buf[0]
    a2 = net.start(tmp.at[0], buf.at[4], to(right))
    b0.wait_recv()
    tmp[1] = src(left, 1)[...] + buf[1]
    b2 = net.start(tmp.at[1], buf.at[5], to(left))
    ready(me)
    yield
    a1.wait_recv()
    b1.wait_recv()
    a2.wait_recv()
    store(0, src(me, 0)[...] + (buf[3] + buf[4]))
    b2.wait_recv()
    store(1, src(me, 1)[...] + (buf[2] + buf[5]))


def scatter_rows(net, part_ref, refs, where, to_z, to_x, other_core, out):
    z, x, core = where
    buf_ref, tmp_ref, r0_ref, c1_ref, c2_ref, rz_ref = refs
    right, left, opp = ring4(x)
    crossing = []
    for p in (opp, right, left, x):
        src = part_ref.at[:, lax.div(p, 2), lax.rem(p, 2), 1 - core]
        crossing.append(net.start(src, r0_ref.at[p], other_core))
    arriving = iter(crossing)
    yield

    def ready(p):
        next(arriving).wait_recv()
        c1_ref[p] = part_ref[:, lax.div(p, 2), lax.rem(p, 2), core] + r0_ref[p]

    def store(h, value):
        c2_ref[pl.ds(h * (NZ // 2), NZ // 2)] = value

    def src(p, h):
        return c1_ref.at[p, pl.ds(h * (NZ // 2), NZ // 2)]

    yield from scatter4(net, src, x, to_x, buf_ref, tmp_ref, store, ready)
    copies = []
    for d in range(1, NZ):
        p = lax.rem(z + d, NZ)
        copies.append(net.start(c2_ref.at[p], rz_ref.at[d - 1], to_z(p)))
    yield
    total = c2_ref[z]
    for d, copy in enumerate(copies):
        copy.wait_recv()
        total = total + rz_ref[d]
    out.append(total)


def gram_sum(net, share, refs, where, to_z, to_xy, other_core):
    g_ref, g0_ref, s0_ref, g1_ref, g2_ref, gf_ref = refs
    z, w, core = where
    gram = lax.dot_general(
        share, share, (((0,), (0,)), ((), ())), precision=HI, preferred_element_type=F32
    )
    g_ref[0] = gram[:, :128]
    g_ref[1] = gram[:, 128:]
    crossing = net.start(g_ref.at[1 - core], g0_ref, other_core)
    yield
    crossing.wait_recv()
    s0_ref[...] = g_ref[core] + g0_ref[...]

    def piece(p):
        return pl.ds(pl.multiple_of(p * THIN, THIN), THIN)

    others = [lax.rem(w + d, NX * NY) for d in range(1, NX * NY)]
    copies = [net.start(s0_ref.at[piece(p)], g1_ref.at[d], to_xy(p)) for d, p in enumerate(others)]
    yield
    total = s0_ref[piece(w)]
    for d, copy in enumerate(copies):
        copy.wait_recv()
        total = total + g1_ref[d]
    g2_ref[z] = total
    spot = g2_ref.at[z]
    copies = [net.start(spot, spot, to_z(lax.rem(z + d, NZ))) for d in range(1, NZ)]
    yield
    for copy in copies:
        copy.wait_recv()
    total = g2_ref[0]
    for d in range(1, NZ):
        total = total + g2_ref[d]
    gf_ref[core, piece(w)] = total
    spot = gf_ref.at[core, piece(w)]
    copies = [net.start(spot, spot, to_xy(p)) for p in others]
    yield
    for copy in copies:
        copy.wait_recv()
    spot = gf_ref.at[core]
    crossing = net.start(spot, spot, other_core)
    yield
    crossing.wait_recv()


def tile_products(tiles_ref, order_ref, load, prefix_ref, store, transposed, twice):
    dn = (((0,), (0,)), ((), ())) if transposed else (((1,), (0,)), ((), ()))

    def step(k, acc):
        tile = tiles_ref[order_ref[k]]
        if twice:
            tile = jnp.concatenate([tile, tile], axis=0 if transposed else 1)
        prod = lax.dot_general(tile, load(order_ref[32 + k]), dn, preferred_element_type=F32)
        acc = acc * order_ref[64 + k].astype(F32) + prod
        prefix_ref[k] = acc
        return acc

    lax.fori_loop(0, SLOTS, step, jnp.zeros((TILE, W), F32), unroll=8)
    for b in range(TR):
        store(b, prefix_ref[order_ref[96 + b]] * order_ref[112 + b].astype(F32))


def two_parts(value):
    high = value.astype(BF16)
    return high, (value - high.astype(F32)).astype(BF16)


def step(*running):
    for stage in running:
        next(stage, None)


def scratch_shapes():
    shapes = {
        "x_first0": ((NZ, 2, 2, 2, 1, 32, W), BF16),
        "x_first1": ((NZ, 2, 2, 2, 1, 32, W), BF16),
        "x_rows0": ((NZ, 2, 2, 2, 2, 32, W), BF16),
        "x_rows1": ((NZ, 2, 2, 2, 2, 32, W), BF16),
        "x_columns0": ((NY, 2, 2, 2, TILE, W), BF16),
        "x_columns1": ((NY, 2, 2, 2, TILE, W), BF16),
        "tiles": ((SLOTS, TILE, TILE), BF16),
        "prefix": ((SLOTS, TILE, W), F32),
        "part_rows": ((2, NY, 2, 2, TILE, W), F32),
        "part_columns": ((2, NZ, 2, 2, 2, 32, W), F32),
        "buf_rows": ((2, 6, 2, TILE, W), F32),
        "tmp_rows": ((2, 2, 2, TILE, W), F32),
        "buf_columns": ((2, 6, NZ // 2, 32, W), F32),
        "tmp_columns": ((2, 2, NZ // 2, 32, W), F32),
        "r0": ((2, NX, NZ, 32, W), F32),
        "c1": ((2, NX, NZ, 32, W), F32),
        "c2": ((2, NZ, 32, W), F32),
        "rz": ((2, NZ - 1, 32, W), F32),
        "g": ((2, 2, K, 128), F32),
        "g0": ((2, K, 128), F32),
        "s0": ((2, K, 128), F32),
        "g1": ((2, NX * NY - 1, THIN, 128), F32),
        "g2": ((2, NZ, THIN, 128), F32),
        "gf": ((2, 2, K, 128), F32),
        "a": ((K, K), F32),
        "e": ((K, K), F32),
        "u": ((K, K), F32),
        "inverse": ((K, K), F32),
        "y_share": ((4 * TILE, K), F32),
        "z_share": ((32, K), F32),
    }
    return {name: VM(shape, dtype) for name, (shape, dtype) in shapes.items()}


FIRST, COLUMNS, ROWS, LAST = 0, 60, 160, 260
COPIES = 310


def power_kernel(
    row_scale, column_scale, sketch_ref, stored_ref, byrow_ref, bycol_ref, share_ref, gram_ref, *refs
):
    send, recv, tiles_sem = refs[:3]
    ref = dict(zip(scratch_shapes(), refs[3:]))
    tiles_ref = ref["tiles"]
    fetch = pltpu.make_async_copy(stored_ref, tiles_ref, tiles_sem)
    fetch.start()
    row, y = lax.axis_index("rows"), lax.axis_index("cols")
    core = lax.rem(row, 2)
    x = lax.rem(lax.div(row, 2), NX)
    z = lax.div(row, 2 * NX)
    q = lax.rem(row, 2 * NX)
    w = x * NY + y

    def at(z_, q_, y_):
        return (z_ * (2 * NX) + q_, y_)

    to_z = lambda p: at(p, q, y)
    to_xy = lambda p: at(z, lax.div(p, NY) * 2 + core, lax.rem(p, NY))
    to_x = lambda p: at(z, p * 2 + core, y)
    to_y = lambda p: at(z, q, p)
    other_core = at(z, x * 2 + (1 - core), y)

    barrier = pltpu.get_barrier_semaphore()
    for d in range(1, NZ):
        pl.semaphore_signal(barrier, 1, device_id=to_z(lax.rem(z + d, NZ)), device_id_type=MESH)
    for d in range(1, NX * NY):
        other = to_xy(lax.rem(w + d, NX * NY))
        pl.semaphore_signal(barrier, 1, device_id=other, device_id_type=MESH)
    pl.semaphore_signal(barrier, 1, device_id=other_core, device_id_type=MESH)
    pl.semaphore_wait(barrier, NZ - 1 + NX * NY - 1 + 1)

    def gram_of(net, share, parity):
        refs = [ref[name].at[parity] for name in ("g", "g0", "s0", "g1", "g2", "gf")]
        return gram_sum(net, share, refs, (z, w, core), to_z, to_xy, other_core)

    def half_columns(net, h, value, out):
        xs, part = ref["x_columns" + str(h)], ref["part_columns"].at[h]
        for i, v in enumerate(value):
            xs[y, :, :, i] = v.reshape(2, 2, TILE, W)
        gather = gather4(net, lambda p, i: xs.at[p, i], y, to_y)
        names = ("buf_columns", "tmp_columns", "r0", "c1", "c2", "rz")
        buffers = [ref[name].at[h] for name in names]
        scatter = scatter_rows(net, part, buffers, (z, x, core), to_z, to_x, other_core, out)

        def load(b):
            return xs[b >> 2, (b >> 1) & 1, b & 1].reshape(2 * TILE, W)

        def keep(b, value):
            part[b // 2, b % 2] = value.reshape(2, 2, 32, W)

        def products():
            tile_products(tiles_ref, bycol_ref, load, ref["prefix"], keep, True, True)

        return gather, products, scatter

    def half_rows(net, h, value, out):
        xs = ref[("x_first" if len(value) == 1 else "x_rows") + str(h)]
        part = ref["part_rows"].at[h]
        for i, v in enumerate(value):
            xs[z, lax.div(x, 2), lax.rem(x, 2), core, i] = v
        gather = gather_rows(net, xs, (z, x, core), to_z, to_x, other_core)

        def store(i, value):
            out.append(value.reshape(2 * TILE, W))

        scatter = scatter4(
            net,
            lambda p, i: part.at[p, i],
            y,
            to_y,
            ref["buf_rows"].at[h],
            ref["tmp_rows"].at[h],
            store,
        )

        def load(b):
            both = xs[b >> 1, b & 1]
            parts = [both[:, :, i].reshape(TILE, W) for i in range(both.shape[2])]
            return parts[0] if len(parts) == 1 else jnp.concatenate(parts, axis=0)

        def keep(b, value):
            part[b // 4, (b // 2) % 2, b % 2] = value

        def products():
            tile_products(tiles_ref, byrow_ref, load, ref["prefix"], keep, False, len(value) == 2)

        return gather, products, scatter

    def panel(i):
        factor_panel(i * PANEL, ref["a"], ref["e"], ref["u"], ref["inverse"])

    def factor_begin(scale, parity):
        full = jnp.concatenate([ref["gf"][parity, 0], ref["gf"][parity, 1]], axis=1)
        factor_start(full * scale, ref["a"], ref["e"], ref["u"], ref["inverse"])

    def put(out, share):
        for i, halves in enumerate(zip(*out)):
            value = apply_inverse(jnp.concatenate(halves, axis=1), ref["inverse"][...])
            share[i * value.shape[0] : (i + 1) * value.shape[0], :] = value

    def first():
        net, out = Net(send, recv, FIRST), ([], [])
        g0, p0, s0 = half_rows(net, 0, (sketch_ref[:, :W],), out[0])
        g1, p1, s1 = half_rows(net, 1, (sketch_ref[:, W:],), out[1])
        step(g0, g0, g1, g0, g1, g0)
        fetch.wait()
        p0()
        step(s0, g1, g1)
        p1()
        step(s1, s0, s1, s0, s1)
        for h in range(2):
            for i in range(2):
                ref["y_share"][i * 2 * TILE : (i + 1) * 2 * TILE, h * W : (h + 1) * W] = out[h][i]
        net.drain()

    def columns():
        net, out = Net(send, recv, COLUMNS), ([], [])
        share = ref["y_share"]
        gram = gram_of(net, share[...], 0)
        g0, p0, s0 = half_columns(net, 0, two_parts(share[:, :W]), out[0])
        g1, p1, s1 = half_columns(net, 1, two_parts(share[:, W:]), out[1])
        step(g0, gram, gram, g0, g1, gram, g0)
        p0()
        step(s0, g1, gram, s0, g1)
        p1()
        step(s1, gram, s0, s1, gram)
        factor_begin(row_scale, 0)
        panel(0)
        step(s0, s1)
        panel(1)
        step(s1)
        panel(2)
        panel(3)
        step(s0, s1)
        put(out, ref["z_share"])
        net.drain()

    def rows():
        net, out = Net(send, recv, ROWS), ([], [])
        share = ref["z_share"]
        gram = gram_of(net, share[...], 1)
        g0, p0, s0 = half_rows(net, 0, two_parts(share[:, :W]), out[0])
        g1, p1, s1 = half_rows(net, 1, two_parts(share[:, W:]), out[1])
        step(g0, gram, g0, g1, gram, g0, gram, g0)
        p0()
        step(s0, g1, gram, g1, s0, gram, g1)
        p1()
        step(s1, gram)
        factor_begin(column_scale, 1)
        panel(0)
        panel(1)
        step(s0, s1)
        panel(2)
        panel(3)
        step(s1)
        put(out, ref["y_share"])
        net.drain()

    def one_round(i, carry):
        columns()
        rows()
        return carry

    first()
    lax.fori_loop(0, ROUNDS, one_round, 0)
    net = Net(send, recv, LAST)
    for stage in gram_of(net, ref["y_share"][...], 0):
        pass
    share_ref[...] = ref["y_share"][...]
    gram_ref[:, :128] = ref["gf"][0, 0]
    gram_ref[:, 128:] = ref["gf"][0, 1]
    net.drain()


def power(sketch, tiles, by_row, by_col, row_scale, column_scale):
    vmem, smem = pl.BlockSpec(memory_space=VM), pl.BlockSpec(memory_space=pltpu.SMEM)
    return pl.pallas_call(
        functools.partial(power_kernel, row_scale, column_scale),
        name="power",
        out_shape=(
            jax.ShapeDtypeStruct((4 * TILE, K), F32),
            jax.ShapeDtypeStruct((K, K), F32),
        ),
        in_specs=[vmem, pl.BlockSpec(memory_space=pl.ANY), smem, smem],
        out_specs=[vmem, vmem],
        scratch_shapes=[pltpu.SemaphoreType.DMA((COPIES,))] * 2
        + [pltpu.SemaphoreType.DMA]
        + list(scratch_shapes().values()),
        compiler_params=pltpu.CompilerParams(
            collective_id=1, has_side_effects=True, vmem_limit_bytes=48 * MIB
        ),
    )(sketch, tiles, by_row, by_col)


def shards(tiles, tile_rows, tile_cols, tile_counts, sketch):
    row_scale = 1.0 / (TR * TILE * lax.axis_size("rows"))
    column_scale = 1.0 / (CGT * TILE * lax.axis_size("cols"))
    by_row, by_col = slot_orders(tile_rows[0, 0], tile_cols[0, 0], tile_counts[0])
    share, gram = power(sketch[0], tiles[0, 0], by_row, by_col, row_scale, column_scale)
    return factorize(gram, row_scale, share)


def solution(mesh):
    return jax.shard_map(
        shards,
        mesh=mesh,
        in_specs=(
            P("rows", "cols", None, None, None),
            P("rows", "cols", None),
            P("rows", "cols", None),
            P("rows", "cols"),
            P("cols", "rows", None),
        ),
        out_specs=(P(("rows", "cols"), None), P()),
        check_vma=False,
    )
```
